128 devices in a mesh: lon: 32 (over x, z, y_hi), grp: 4 (over y_lo, core).
Axes of the slice: x: 4, y: 4 (y_hi: 2, y_lo: 2; y = y_hi * 2 + y_lo), z: 4, core: 2. Of those that a mesh axis runs over, the one named last changes fastest.
Arguments:
- features: bfloat16 [64, 4096, 128], P('grp', 'lon'), may hold values from -6 to 6
- conv_one_w: bfloat16 [3, 3, 128, 128], replicated, may hold values from -0.1875 to 0.1875
- conv_one_b: float32 [128], replicated, may hold values from -3 to 3
- conv_two_w: bfloat16 [3, 3, 128, 128], replicated, may hold values from -0.1875 to 0.1875
- conv_two_b: float32 [128], replicated, may hold values from -3 to 3
- out_conv_w: bfloat16 [3, 3, 128, 3], replicated, may hold values from -0.1875 to 0.1875
- out_conv_b: float32 [3], replicated, may hold values from -3 to 3
- vgg_one_w: bfloat16 [64, 3, 3, 3], replicated, may hold values from -1.25 to 1.25
- vgg_one_b: float32 [64], replicated, may hold values from -3 to 3
- vgg_two_w: bfloat16 [64, 64, 3, 3], replicated, may hold values from -0.25 to 0.25
- vgg_two_b: float32 [64], replicated, may hold values from -3 to 3
- lin_weights: float32 [64], replicated, may hold values from 0.1 to 1
- row_lists: int32 [128, 3, 8], P(('lon', 'grp')), may hold values from 0 to 15, as said below
- tap_index: int32 [128, 4, 8192], P(('lon', 'grp')), may hold values from 0 to 3071, as said below
- tap_weight: float32 [128, 4, 8192], P(('lon', 'grp')), may hold values from 0 to 1, as said below
- target_tiles: bfloat16 [128, 3, 64, 128], P(('lon', 'grp')), may hold values from -3 to 3
Outputs:
- loss: float32 [], replicated
- grad_one: float32 [3, 3, 128, 128], replicated
- grad_two: float32 [3, 3, 128, 128], replicated
- grad_out: float32 [3, 3, 128, 3], replicated
The draws below stay inside these ranges and needn't reach their ends.
Inputs may be any that keep to these rules, and one draw needn't show every extreme that they name: `row_lists`: each list is 8 consecutive rows of the sending slab, and the three slabs that serve one tile send the same rows. `tap_index`: the four taps of a pixel are the corners of one cell: slots j and j + 1 of one offset, columns x and x + 1 of the three slabs laid side by side from west to east. `tap_weight`: the four weights of a pixel are the bilinear weights of that cell: non-negative, summing to one.
All inputs are finite; a program needn't handle non-finite values.
Results may differ from the reference program's by a relative error of at most 0.0055.
Values may be sent and summed in bfloat16 or wider, within the bound.
A program may use at most 128 MiB of HBM per device.

```python
import math
import jax
import jax.numpy as jnp
from jax import lax

CH = 128
VW = 64
COLS_DEV = 128
ROWS_DEV = 16
TILE_H = 64
TILE_W = 128
SLOTS = 8
NROWS = 64
NCOLS = 4096
N_LON = 32
N_GRP = 4
DEVICES = 128


def tile_plan(key):
    grp_total = NROWS // ROWS_DEV
    owners = jnp.arange(DEVICES, dtype=jnp.int32)
    grp_of = owners % grp_total
    polar = (grp_of == 0) | (grp_of == grp_total - 1)
    key_one, key_two, key_three, key_four = jax.random.split(key, 4)
    wide_base = jax.random.randint(key_one, (DEVICES,), 110, 151)
    narrow_base = jax.random.randint(key_two, (DEVICES,), 64, 121)
    base = jnp.where(polar, wide_base, narrow_base).astype(jnp.int32)
    slope = jax.random.randint(key_three, (DEVICES,), 0, 30).astype(jnp.int32)
    starts = jax.random.randint(key_four, (DEVICES,), 0, ROWS_DEV - SLOTS + 1).astype(jnp.int32)
    starts = starts.at[0].set(ROWS_DEV - SLOTS).at[1].set(0)
    return (base, slope, starts)


def pixel_taps(base, slope):
    rows = jnp.arange(TILE_H, dtype=jnp.int32)
    cols = jnp.arange(TILE_W, dtype=jnp.int32)
    factor = base[:, None] + slope[:, None] * (2 * rows[None, :] + 1) // (2 * TILE_H)
    spanq = (2 * cols[None, None, :] + 1 - TILE_W) * COLS_DEV * factor[:, :, None]
    xq = 128 * (COLS_DEV + COLS_DEV // 2) + spanq // TILE_W
    yq = (2 * rows + 1) * (SLOTS - 1) * 64 // TILE_H
    x_low = xq // 128
    frac_x = (xq - 128 * x_low).astype(jnp.float32) / 128.0
    y_low = jnp.minimum(yq // 128, SLOTS - 2)
    frac_y = ((yq - 128 * y_low).astype(jnp.float32) / 128.0)[None, :, None]
    y_low = jnp.broadcast_to(y_low[None, :, None], xq.shape)
    frac_y = jnp.broadcast_to(frac_y, xq.shape)

    def place(y_val, x_val):
        return (x_val // COLS_DEV * SLOTS + y_val) * COLS_DEV + x_val % COLS_DEV
    index = jnp.stack([place(y_low, x_low), place(y_low, x_low + 1), place(y_low + 1, x_low), place(y_low + 1, x_low + 1)], axis=1)
    weight = jnp.stack([(1.0 - frac_y) * (1.0 - frac_x), (1.0 - frac_y) * frac_x, frac_y * (1.0 - frac_x), frac_y * frac_x], axis=1)
    return (index.reshape(DEVICES, 4, TILE_H * TILE_W).astype(jnp.int32), weight.reshape(DEVICES, 4, TILE_H * TILE_W).astype(jnp.float32))


def draw_row_lists(key, part):
    base, slope, starts = tile_plan(key)
    grp_total = NROWS // ROWS_DEV
    lon_total = NCOLS // COLS_DEV
    source = jnp.arange(DEVICES, dtype=jnp.int32)
    source_lon = source // grp_total
    source_grp = source % grp_total
    offsets = jnp.arange(3, dtype=jnp.int32)
    owner = (source_lon[:, None] + 1 - offsets[None, :]) % lon_total * grp_total + source_grp[:, None]
    rows = starts[owner][:, :, None] + jnp.arange(SLOTS, dtype=jnp.int32)[None, None, :]
    return rows.astype(jnp.int32)


def draw_tap_index(key, part):
    base, slope, starts = tile_plan(key)
    return pixel_taps(base, slope)[0]


def draw_tap_weight(key, part):
    base, slope, starts = tile_plan(key)
    return pixel_taps(base, slope)[1]


def block_scale(own_key, dims, cuts, smallest, top_value):
    factor_of, own = 1.0, jax.random.fold_in(own_key, 6)
    for position, blocks in cuts:
        heights = jnp.exp(jax.random.uniform(jax.random.fold_in(own, position), (blocks,), jnp.float32, smallest / len(cuts), top_value / len(cuts)))
        factor_of = factor_of * jnp.repeat(heights, dims[position] // blocks).reshape([-1 if axis == position else 1 for axis in range(len(dims))])
    return factor_of


def noise(own_key, shape, deviation, most, cuts=(), held_as=jnp.bfloat16):
    result = deviation * jax.random.normal(own_key, shape, jnp.float32)
    if cuts:
        result = result * block_scale(own_key, shape, cuts, -0.22, 0.18)
    return jnp.clip(result, -most, most).astype(held_as)


def setup_inputs(seed: int = 0) -> dict:
    splits = jax.random.split(jax.random.key(seed), 17)
    return {
        "features": noise(splits[0], (NROWS, NCOLS, CH), 1.0, 6.0, ((0, 4), (1, 32))),
        "conv_one_w": noise(splits[1], (3, 3, CH, CH), (9 * CH) ** -0.5, 0.1875),
        "conv_one_b": noise(splits[2], (CH,), 0.3, 3.0, (), jnp.float32),
        "conv_two_w": noise(splits[3], (3, 3, CH, CH), (9 * CH) ** -0.5, 0.1875),
        "conv_two_b": noise(splits[4], (CH,), 0.3, 3.0, (), jnp.float32),
        "out_conv_w": noise(splits[5], (3, 3, CH, 3), (9 * CH) ** -0.5, 0.1875),
        "out_conv_b": noise(splits[6], (3,), 0.3, 3.0, (), jnp.float32),
        "vgg_one_w": noise(splits[7], (VW, 3, 3, 3), 27 ** -0.5, 1.25),
        "vgg_one_b": noise(splits[8], (VW,), 0.3, 3.0, (), jnp.float32),
        "vgg_two_w": noise(splits[9], (VW, VW, 3, 3), (9 * VW) ** -0.5, 0.25),
        "vgg_two_b": noise(splits[10], (VW,), 0.3, 3.0, (), jnp.float32),
        "lin_weights": jnp.clip(jnp.exp(jax.random.uniform(splits[11], (VW,), jnp.float32, math.log(0.1), math.log(1.0))), 0.1, 1.0),
        "row_lists": draw_row_lists(jax.random.fold_in(splits[16], 71), 0),
        "tap_index": draw_tap_index(jax.random.fold_in(splits[16], 71), 0),
        "tap_weight": draw_tap_weight(jax.random.fold_in(splits[16], 71), 0),
        "target_tiles": noise(splits[15], (DEVICES, 3, TILE_H, TILE_W), 0.5, 3.0, ((0, 128),)),
    }


offset_rgb = (-0.03, -0.088, -0.188)
spread_rgb = (0.458, 0.448, 0.45)
loss_scale = 64.0

def conv_valid(padded, weight):
    return lax.conv_general_dilated(padded[None], weight, (1, 1), 'VALID', dimension_numbers=('NHWC', 'HWIO', 'NHWC'), preferred_element_type=jnp.float32)[0]

def conv_same(picture, weight):
    return lax.conv_general_dilated(picture[None], weight, (1, 1), 'SAME', dimension_numbers=('NCHW', 'OIHW', 'NCHW'), preferred_element_type=jnp.float32)[0]

def flip_weight(weight):
    return jnp.transpose(weight[::-1, ::-1], (0, 1, 3, 2))

def weight_grad(padded, adjoint):
    height, breadth, out_channels = adjoint.shape
    in_channels = padded.shape[2]
    flat_adjoint = adjoint.reshape(height * breadth, out_channels)
    pieces = []
    for offset_y in range(3):
        for offset_x in range(3):
            window = padded[offset_y:offset_y + height, offset_x:offset_x + breadth].reshape(height * breadth, in_channels)
            pieces.append(lax.dot_general(window, flat_adjoint, (((0,), (0,)), ((), ())), preferred_element_type=jnp.float32))
    return jnp.stack(pieces).reshape(3, 3, in_channels, out_channels)

def silu_slope(hidden):
    hidden_f32 = hidden.astype(jnp.float32)
    sigmoid_val = jax.nn.sigmoid(hidden_f32)
    return sigmoid_val * (1.0 + hidden_f32 * (1.0 - sigmoid_val))

def silu_round(hidden):
    return jax.nn.silu(hidden.astype(jnp.float32)).astype(jnp.bfloat16)

def decoder_forward(features, conv_one_w, conv_one_b, conv_two_w, conv_two_b, out_conv_w, out_conv_b, padder):
    pad_zero = padder(silu_round(features))
    hidden_one = (conv_valid(pad_zero, conv_one_w) + conv_one_b).astype(jnp.bfloat16)
    pad_one = padder(silu_round(hidden_one))
    hidden_two = (features.astype(jnp.float32) + conv_valid(pad_one, conv_two_w) + conv_two_b).astype(jnp.bfloat16)
    pad_two = padder(silu_round(hidden_two))
    colour = conv_valid(pad_two, out_conv_w) + out_conv_b
    return (colour, (pad_zero, hidden_one, pad_one, hidden_two, pad_two))

def decoder_backward(colour_adj, saved, conv_two_w, out_conv_w, padder):
    pad_zero, hidden_one, pad_one, hidden_two, pad_two = saved
    adj_three = colour_adj.astype(jnp.bfloat16)
    grad_out = weight_grad(pad_two, adj_three)
    adj_two = (conv_valid(padder(adj_three), flip_weight(out_conv_w)) * silu_slope(hidden_two)).astype(jnp.bfloat16)
    grad_two = weight_grad(pad_one, adj_two)
    adj_one = (conv_valid(padder(adj_two), flip_weight(conv_two_w)) * silu_slope(hidden_one)).astype(jnp.bfloat16)
    grad_one = weight_grad(pad_zero, adj_one)
    return (grad_one, grad_two, grad_out)

def vgg_block(picture, vgg_one_w, vgg_one_b, vgg_two_w, vgg_two_b):
    offset = jnp.array(offset_rgb, jnp.float32)[:, None, None]
    spread = jnp.array(spread_rgb, jnp.float32)[:, None, None]
    scaled = ((picture.astype(jnp.float32) - offset) / spread).astype(jnp.bfloat16)
    first_layer = jax.nn.relu(conv_same(scaled, vgg_one_w) + vgg_one_b[:, None, None]).astype(jnp.bfloat16)
    return jax.nn.relu(conv_same(first_layer, vgg_two_w) + vgg_two_b[:, None, None])

def unit_norm(feature):
    return feature * lax.rsqrt(lax.optimization_barrier(jnp.sum(feature * feature, axis=0, keepdims=True)) + 1e-05)

def tile_loss(predicted, target, vgg_one_w, vgg_one_b, vgg_two_w, vgg_two_b, lin_weights):
    height, breadth = (target.shape[1], target.shape[2])
    pred_feat = vgg_block(predicted.reshape(3, height, breadth), vgg_one_w, vgg_one_b, vgg_two_w, vgg_two_b)
    true_feat = vgg_block(target, vgg_one_w, vgg_one_b, vgg_two_w, vgg_two_b)
    difference = unit_norm(pred_feat) - unit_norm(true_feat)
    return jnp.mean(lax.optimization_barrier(jnp.sum(lin_weights[:, None, None] * difference * difference, axis=0)))

def pad_cycle(grid_field):
    widened = jnp.concatenate([grid_field[:, -1:], grid_field, grid_field[:, :1]], axis=1)
    zero_row = jnp.zeros_like(widened[:1])
    return jnp.concatenate([zero_row, widened, zero_row], axis=0)

def reference(features, conv_one_w, conv_one_b, conv_two_w, conv_two_b, out_conv_w, out_conv_b, vgg_one_w, vgg_one_b, vgg_two_w, vgg_two_b, lin_weights, row_lists, tap_index, tap_weight, target_tiles):
    colour, saved = decoder_forward(features, conv_one_w, conv_one_b, conv_two_w, conv_two_b, out_conv_w, out_conv_b, pad_cycle)
    picture = jnp.transpose(colour, (0, 2, 1))

    def total_loss(picture_in):

        def one_tile(owner):
            owner_lon = owner // N_GRP
            owner_grp = owner % N_GRP
            block_index = tap_index[owner] // COLS_DEV
            column = tap_index[owner] % COLS_DEV
            offset_k = block_index // SLOTS
            slot_index = block_index % SLOTS
            source_lon = (owner_lon + offset_k - 1) % N_LON
            source = (source_lon * N_GRP + owner_grp).astype(jnp.int32)
            local_row = row_lists[source, offset_k, slot_index]
            glob_row = (owner_grp * ROWS_DEV + local_row).astype(jnp.int32)
            glob_col = (source_lon * COLS_DEV + column).astype(jnp.int32)
            values = picture_in[glob_row, :, glob_col]
            predicted = lax.optimization_barrier(jnp.sum(values * tap_weight[owner][:, :, None], axis=0)).T
            return tile_loss(predicted, target_tiles[owner], vgg_one_w, vgg_one_b, vgg_two_w, vgg_two_b, lin_weights)
        return jnp.sum(lax.map(one_tile, jnp.arange(DEVICES, dtype=jnp.int32)))
    loss, pullback = jax.vjp(total_loss, picture)
    picture_adj, = pullback(jnp.ones_like(loss) * loss_scale)
    colour_adj = jnp.transpose(picture_adj, (0, 2, 1))
    grad_one, grad_two, grad_out = decoder_backward(colour_adj, saved, conv_two_w, out_conv_w, pad_cycle)
    return (loss, grad_one, grad_two, grad_out)
```

```python
import jax
import jax.numpy as jnp
from jax import lax
from jax.experimental import pallas as pl
from jax.experimental.pallas import tpu as pltpu
from jax.sharding import PartitionSpec as P

OFFSET = (-0.03, -0.088, -0.188)
SPREAD = (0.458, 0.448, 0.45)
LOSS_SCALE = 64.0

CH = 128
VW = 64
ROWS = 16
COLS = 128
WIDE = 160
TROWS = 64
PIX = TROWS * 128
BF = jnp.bfloat16
F32 = jnp.float32
MESH = pl.DeviceIdType.MESH

AROUND = ((-1, -1), (-1, 0), (-1, 1), (0, -1), (0, 1), (1, -1), (1, 0), (1, 1))


def dot(a, b, ca=1, cb=0):
    return lax.dot_general(a, b, (((ca,), (cb,)), ((), ())), preferred_element_type=F32)


def span(start, size, unit):
    if isinstance(start, int):
        return pl.ds(start, size)
    return pl.ds(pl.multiple_of(start, unit), size)


def ext(delta, low, high):
    return low if delta < 0 else high


def conv_rows(src, weight, r, n, last=0):
    lhs = jnp.concatenate(
        [src[pl.ds(r + a, n)].reshape(n * WIDE, CH) for a in range(3)], axis=1
    )
    z = dot(lhs, weight, 1, last)
    return (
        pltpu.roll(z[:, :CH], 1, 0)
        + z[:, CH : 2 * CH]
        + pltpu.roll(z[:, 2 * CH :], n * WIDE - 1, 0)
    )


def act_slope(hidden):
    h = hidden.astype(F32)
    s = jax.nn.sigmoid(h)
    return (h * s).astype(BF), s * (1.0 + h * (1.0 - s))


def lane_masks(n):
    col = lax.broadcasted_iota(jnp.int32, (1, 128), 1)
    return col > 0, col < 127


def shift_store(ref, y, row0, n):
    first, last = lane_masks(n)
    for r in range(n):
        part = y[:, r * 128 : (r + 1) * 128]
        at = span((row0 + r + 1) * 128, 128, 128)
        ref[0, :, at] = jnp.where(first, pltpu.roll(part, 1, 1), 0.0).astype(BF)
        ref[1, :, at] = part.astype(BF)
        ref[2, :, at] = jnp.where(last, pltpu.roll(part, 127, 1), 0.0).astype(BF)


def per_channel(values):
    row = lax.broadcasted_iota(jnp.int32, (8, 1), 0)
    out = jnp.full((8, 1), values[2], F32)
    out = jnp.where(row == 0, values[0], out)
    return jnp.where(row == 1, values[1], out)


def store_scaled(zs, colours, row0, n):
    row = lax.broadcasted_iota(jnp.int32, (8, 1), 0)
    z = jnp.where(row < 3, (colours - per_channel(OFFSET)) / per_channel(SPREAD), 0.0)
    first, last = lane_masks(n)
    for r in range(n):
        part = z[:, r * 128 : (r + 1) * 128]
        stack = jnp.concatenate(
            [
                jnp.where(first, pltpu.roll(part, 1, 1), 0.0),
                part,
                jnp.where(last, pltpu.roll(part, 127, 1), 0.0),
                jnp.zeros_like(part),
            ],
            axis=0,
        )
        zs[:, span((row0 + r + 1) * 128, 128, 128)] = stack.astype(BF)


def vgg_first(zs, fs, v1, v1b, n):
    @pl.loop(0, TROWS // n)
    def _(k):
        r0 = k * n
        rhs = jnp.concatenate(
            [zs[:, span((r0 + a) * 128, n * 128, 128)] for a in range(3)], axis=0
        )
        y = jnp.maximum(dot(v1, rhs) + v1b, 0.0)
        shift_store(fs, y, r0, n)


def nine_taps(ref, r0, n):
    return jnp.concatenate(
        [ref[b, :, span((r0 + a) * 128, n * 128, 128)] for a in range(3) for b in range(3)], axis=0
    )


def inv_norm(f):
    return lax.rsqrt(jnp.sum(f * f, axis=0, keepdims=True) + 1e-05)


def kernel(
    feat, w1, b1, w2, b2, wo, bo, v1w, v1b, v2w, v2b, lin, rows_ref, tap_i, tap_w, target,
    grads, loss_out,
    f_ref, a0, a1, a2, s1, s2, w1c, w2c, w2f, c_own, c_near, hot, al, ar, v1f, v2c, v2t,
    zs, fs, gs, unit_t, y_ref, tb, pb, ca, ca_near, own_e, all_e, d2, d1, t0, t1, loss_acc, wof,
    halo_send, halo_recv, col_send, col_recv, tab_send, tab_recv, adj_send, adj_recv,
):
    lon, grp = lax.axis_index("lon"), lax.axis_index("grp")
    n_lon, n_grp = lax.axis_size("lon"), lax.axis_size("grp")

    def near(dl, dg):
        return (lax.rem(lon + dl + n_lon, n_lon), lax.rem(grp + dg + n_grp, n_grp))

    barrier = pltpu.get_barrier_semaphore()
    for dl, dg in AROUND:
        pl.semaphore_signal(barrier, inc=1, device_id=near(dl, dg), device_id_type=MESH)

    for a in range(3):
        for b in range(3):
            rows, cols = slice(a * CH, (a + 1) * CH), slice(b * CH, (b + 1) * CH)
            w1c[rows, cols] = w1[a, b]
            w2c[rows, cols] = w2[a, b]
            w2f[cols, rows] = w2[2 - a, 2 - b]
    v1f[...] = jnp.zeros_like(v1f)
    wof[...] = jnp.zeros_like(wof)
    for a in range(3):
        for b in range(3):
            for c in range(3):
                v1f[a * 32 + b * 8 + c : a * 32 + b * 8 + c + 1, :] = v1w[c, a, b : b + 1].astype(F32)
            wof[a, b * 8 : b * 8 + 3, :] = wo[a, b].astype(F32)
            v2c[:, (a * 3 + b) * VW : (a * 3 + b + 1) * VW] = v2w[a, b]
            v2t[:, (a * 3 + b) * VW : (a * 3 + b + 1) * VW] = (
                v2w[2 - a, 2 - b].astype(F32).T.astype(BF)
            )
    v1 = v1f[...].T.astype(BF)
    v1b_col = v1b[...].reshape(VW, 1)
    v2b_col = v2b[...].reshape(VW, 1)
    lin_col = lin[...].reshape(VW, 1)

    zs[:, 0:128] = jnp.zeros((32, 128), BF)
    zs[:, PIX + 128 :] = jnp.zeros((32, 128), BF)
    for ref in (fs, gs):
        ref[:, :, 0:128] = jnp.zeros((3, VW, 128), BF)
        ref[:, :, PIX + 128 :] = jnp.zeros((3, VW, 128), BF)
    y_ref[:, 0:128] = jnp.zeros((72, 128), F32)
    y_ref[:, PIX + 128 :] = jnp.zeros((72, 128), F32)
    pb[:, :, 0:8, :] = jnp.zeros((3, 3, 8, 128), F32)
    pb[:, :, 16:24, :] = jnp.zeros((3, 3, 8, 128), F32)
    own_e[...] = jnp.zeros_like(own_e)
    all_e[...] = jnp.zeros_like(all_e)

    pl.semaphore_wait(barrier, len(AROUND))
    take_r = {-1: pl.ds(0, 3), 0: pl.ds(0, ROWS), 1: pl.ds(ROWS - 3, 3)}
    take_c = {-1: pl.ds(0, 16), 0: pl.ds(0, COLS), 1: pl.ds(COLS - 16, 16)}
    land_r = {-1: pl.ds(ROWS + 3, 3), 0: pl.ds(3, ROWS), 1: pl.ds(0, 3)}
    land_c = {-1: pl.ds(COLS + 16, 16), 0: pl.ds(16, COLS), 1: pl.ds(0, 16)}
    halo = []
    for i, (dl, dg) in enumerate(AROUND):
        copy = pltpu.make_async_remote_copy(
            src_ref=feat.at[take_r[dg], take_c[dl]],
            dst_ref=f_ref.at[land_r[dg], land_c[dl]],
            send_sem=halo_send.at[i],
            recv_sem=halo_recv.at[i],
            device_id=near(dl, dg),
            device_id_type=MESH,
        )
        copy.start()
        halo.append(copy)
    f_ref[3 : 3 + ROWS, 16 : 16 + COLS, :] = feat[...]

    for r in range(TROWS):
        tgt = target[:, r, :].astype(F32)
        unit_t[0:8, r * 128 : (r + 1) * 128] = jnp.concatenate(
            [tgt, jnp.zeros((5, 128), F32)], axis=0
        )

    @pl.loop(0, 8)
    def _(k):
        store_scaled(zs, unit_t[0:8, span(k * 1024, 1024, 128)], k * 8, 8)

    vgg_first(zs, fs, v1, v1b_col, 4)

    @pl.loop(0, TROWS // 4)
    def _(k):
        f = jnp.maximum(dot(v2c[...], nine_taps(fs, k * 4, 4)) + v2b_col, 0.0)
        unit_t[:, span(k * 512, 512, 128)] = f * inv_norm(f)

    @pl.loop(0, 8)
    def _(k):
        at = span(k * 1024, 1024, 128)
        index = tap_i[:, at]
        weight = tap_w[:, at]
        column = lax.shift_left(lax.shift_right_logical(index, 10), 7) + jnp.bitwise_and(index, 127)
        slot = jnp.bitwise_and(lax.shift_right_logical(index, 7), 7)
        left = jnp.min(column, axis=0, keepdims=True)
        top = jnp.min(slot, axis=0, keepdims=True)
        is_left, is_top = column == left, slot == top

        def corner(cond):
            return jnp.sum(jnp.where(cond, weight, 0.0), axis=0, keepdims=True)

        not_left, not_top = jnp.logical_not(is_left), jnp.logical_not(is_top)
        w_tl, w_tr = corner(is_top & is_left), corner(is_top & not_left)
        w_bl, w_br = corner(not_top & is_left), corner(not_top & not_left)
        j = lax.broadcasted_iota(jnp.int32, (8, 1024), 0)
        on_top, on_next = j == top, j == top + 1
        al[:, at] = jnp.where(on_top, w_tl, jnp.where(on_next, w_bl, 0.0))
        ar[:, at] = jnp.where(on_top, w_tr, jnp.where(on_next, w_br, 0.0))
        x = lax.broadcasted_iota(jnp.int32, (384, 1024), 0)
        hot[:, at] = jnp.where(x == left, 1.0, 0.0).astype(BF)

    for copy in halo:
        copy.wait()
    north, south = grp == 0, grp == n_grp - 1

    @pl.loop(0, ROWS + 6)
    def _(r):
        a0[r] = act_slope(f_ref[r])[0]

    def clear(ref, rows):
        @pl.when(north)
        def _():
            ref[0:rows] = jnp.zeros((rows, WIDE, CH), BF)

        @pl.when(south)
        def _():
            ref[ref.shape[0] - rows :] = jnp.zeros((rows, WIDE, CH), BF)

    clear(a0, 3)

    @pl.loop(0, 5)
    def _(k):
        r = k * 4
        h = (conv_rows(a0, w1c[...], r, 4) + b1[...]).astype(BF)
        act, slope = act_slope(h)
        a1[pl.ds(r, 4)] = act.reshape(4, WIDE, CH)
        s1[pl.ds(r, 4)] = slope.reshape(4, WIDE, CH)

    clear(a1, 2)

    @pl.loop(0, 6)
    def _(k):
        r = k * 3
        f = f_ref[pl.ds(r + 2, 3)].reshape(3 * WIDE, CH).astype(F32)
        h = (f + conv_rows(a1, w2c[...], r, 3) + b2[...]).astype(BF)
        act, slope = act_slope(h)
        a2[pl.ds(r, 3)] = act.reshape(3, WIDE, CH)
        s2[pl.ds(r, 3)] = slope.reshape(3, WIDE, CH)

    clear(a2, 1)

    wo_cat = jnp.concatenate([wof[a] for a in range(3)], axis=1).astype(BF)
    for r in range(ROWS):
        rhs = jnp.concatenate([a2[r + a] for a in range(3)], axis=1)
        z = dot(wo_cat, rhs, 1, 1)
        colour = z[0:8, 15 : 15 + COLS] + z[8:16, 16 : 16 + COLS] + z[16:24, 17 : 17 + COLS]
        for c in range(3):
            c_own[c, r : r + 1, :] = colour[c : c + 1] + bo[c]

    colours = []
    for i, dl in enumerate((-1, 1)):
        copy = pltpu.make_async_remote_copy(
            src_ref=c_own,
            dst_ref=c_near.at[1 - i],
            send_sem=col_send.at[i],
            recv_sem=col_recv.at[1 - i],
            device_id=near(dl, 0),
            device_id_type=MESH,
        )
        copy.start()
        colours.append(copy)

    for act, turned, first_row in ((a0, t0, 2), (a1, t1, 1)):

        @pl.loop(0, ROWS + 2)
        def _(r, act=act, turned=turned, first_row=first_row):
            block = act[r + first_row].astype(F32).T
            at = span(r * 128, 128, 128)
            for b in range(3):
                turned[b, :, at] = block[:, 15 + b : 15 + b + COLS].astype(BF)

    for copy in colours:
        copy.wait()

    start = rows_ref[0, 1, 0]
    slabs = (c_near.at[0], c_own, c_near.at[1])
    table = jnp.concatenate(
        [
            jnp.concatenate([slab[c, pl.ds(start, 8), :] for c in range(3)], axis=0)
            for slab in slabs
        ],
        axis=1,
    )
    table = jnp.concatenate([table, pltpu.roll(table, 383, 1)], axis=0)
    table_hi = table.astype(BF)
    table_lo = (table - table_hi.astype(F32)).astype(BF)
    table = jnp.concatenate([table_hi, table_lo], axis=0)

    @pl.loop(0, 8)
    def _(k):
        at = span(k * 1024, 1024, 128)
        got = dot(table, hot[:, at])
        got = got[0:48] + got[48:96]
        w_left, w_right = al[:, at], ar[:, at]
        picture = [
            jnp.sum(
                got[c * 8 : c * 8 + 8] * w_left + got[24 + c * 8 : 32 + c * 8] * w_right,
                axis=0,
                keepdims=True,
            )
            for c in range(3)
        ]
        picture = jnp.concatenate(picture + [jnp.zeros((5, 1024), F32)], axis=0)
        store_scaled(zs, picture, k * 8, 8)

    vgg_first(zs, fs, v1, v1b_col, 4)
    loss_acc[...] = jnp.zeros_like(loss_acc)

    @pl.loop(0, TROWS // 4)
    def _(k):
        f = jnp.maximum(dot(v2c[...], nine_taps(fs, k * 4, 4)) + v2b_col, 0.0)
        inv = inv_norm(f)
        u = f * inv
        diff = u - unit_t[:, span(k * 512, 512, 128)]
        weighted = lin_col * diff
        loss_acc[...] += jnp.sum(weighted * diff, axis=0, keepdims=True)
        g = weighted * (2.0 * LOSS_SCALE / PIX)
        g = inv * (g - u * jnp.sum(g * u, axis=0, keepdims=True))
        shift_store(gs, jnp.where(f > 0.0, g, 0.0), k * 4, 4)

    loss = jnp.sum(loss_acc[...], axis=1, keepdims=True) * (1.0 / PIX)
    loss_out[...] = jnp.broadcast_to(loss, (8, 128))

    v1_back = jnp.concatenate(
        [
            v1f[(2 - a) * 32 + (2 - b) * 8 : (2 - a) * 32 + (2 - b) * 8 + 8, :]
            for b in range(3)
            for a in range(3)
        ],
        axis=0,
    ).astype(BF)

    @pl.loop(0, TROWS // 4)
    def _(k):
        g = dot(v2t[...], nine_taps(gs, k * 4, 4)).astype(BF)
        at = span((k * 4 + 1) * 128, 512, 128)
        g = jnp.where(fs[1, :, at] > 0, g, jnp.zeros_like(g))
        y_ref[:, at] = dot(v1_back, g)

    def table_adjoint(k, acc):
        at = span(k * 1024, 1024, 128)
        part = []
        for b in range(3):
            part.append(
                sum(
                    y_ref[(b * 3 + a) * 8 : (b * 3 + a) * 8 + 8, span((k * 8 + a) * 128, 1024, 128)]
                    for a in range(3)
                )
            )
        col = jnp.bitwise_and(lax.broadcasted_iota(jnp.int32, (8, 1024), 1), 127)
        dz = (
            jnp.where(col > 0, pltpu.roll(part[0], 1, 1), 0.0)
            + part[1]
            + jnp.where(col < 127, pltpu.roll(part[2], 1023, 1), 0.0)
        )
        dz = dz.astype(BF).astype(F32) / per_channel(SPREAD)
        spread = jnp.concatenate(
            [w[:, at] * dz[c : c + 1] for w in (al, ar) for c in range(3)], axis=0
        )
        hi = spread.astype(BF)
        lo = (spread - hi.astype(F32)).astype(BF)
        return acc + dot(jnp.concatenate([hi, lo], axis=0), hot[:, at], 1, 1)

    acc = lax.fori_loop(0, 8, table_adjoint, jnp.zeros((96, 384), F32))
    acc = acc[0:48] + acc[48:96]
    adjoint = acc[0:24] + pltpu.roll(acc[24:48], 1, 1)
    for k in range(3):
        for c in range(3):
            tb[k, c] = adjoint[c * 8 : c * 8 + 8, k * 128 : (k + 1) * 128]
    pb[1, :, 8:16, :] = tb[1]

    returned = []
    for i, (k, dl) in enumerate(((0, -1), (2, 1))):
        copy = pltpu.make_async_remote_copy(
            src_ref=tb.at[k],
            dst_ref=pb.at[k, :, pl.ds(8, 8), :],
            send_sem=tab_send.at[i],
            recv_sem=tab_recv.at[i],
            device_id=near(dl, 0),
            device_id_type=MESH,
        )
        copy.start()
        returned.append(copy)
    for copy in returned:
        copy.wait()

    for c in range(3):
        placed = sum(pb[k, c, pl.ds(8 - rows_ref[0, k, 0], ROWS), :] for k in range(3))
        ca[c] = placed.astype(BF)

    exchanged = []
    for i, (dl, dg) in enumerate(AROUND):
        copy = pltpu.make_async_remote_copy(
            src_ref=ca,
            dst_ref=ca_near.at[7 - i],
            send_sem=adj_send.at[i],
            recv_sem=adj_recv.at[7 - i],
            device_id=near(dl, dg),
            device_id_type=MESH,
        )
        copy.start()
        exchanged.append(copy)

    def taps_of(target_e, c, field):
        for b in range(3):
            moved = pltpu.roll(field, 384 - (111 + 2 - b), 1)[:, 0:256]
            target_e[:, b * 8 + c, :] = moved

    def patches(source_e, r):
        return jnp.concatenate([source_e[r + a] for a in range(3)], axis=0)[:, :WIDE].astype(BF)

    rows2 = jnp.zeros((2, 384), F32)
    own = [ca[c].astype(F32) for c in range(3)]
    for c in range(3):
        side = jnp.zeros((ROWS, 128), F32)
        middle = jnp.concatenate([side, own[c], side], axis=1)
        taps_of(own_e, c, jnp.concatenate([rows2, middle, rows2], axis=0))
    grad_out = jnp.zeros((96, CH), F32)
    for r in range(ROWS + 2):
        grad_out += dot(patches(own_e, r), a2[r])
    for a in range(3):
        base = 18 * CH + (2 - a) * 32
        grads[base : base + 32, :] = grad_out[a * 32 : a * 32 + 32]

    for copy in exchanged:
        copy.wait()
    at_of = {delta: i for i, delta in enumerate(AROUND)}
    has_north = jnp.where(north, 0.0, 1.0)
    has_south = jnp.where(south, 0.0, 1.0)
    for c in range(3):

        def line(dg):
            parts = [
                own[c] if (dl, dg) == (0, 0) else ca_near[at_of[(dl, dg)], c].astype(F32)
                for dl in (-1, 0, 1)
            ]
            return jnp.concatenate(parts, axis=1)

        field = jnp.concatenate(
            [line(-1)[ROWS - 2 :] * has_north, line(0), line(1)[0:2] * has_south], axis=0
        )
        taps_of(all_e, c, field)

    wo_flip = jnp.concatenate([wof[2 - a] for a in range(3)], axis=0).astype(BF)
    for r in range(ROWS + 2):
        d2[r] = (dot(patches(all_e, r), wo_flip, 0, 0) * s2[r]).astype(BF)
    clear(d2, 1)

    def weight_grad(turned, adj, base):
        for a in range(3):
            for b in range(3):
                at = base + (a * 3 + b) * CH
                grads[at : at + CH, :] = dot(turned[b, :, a * 128 : a * 128 + ROWS * 128], adj)

    weight_grad(t1, d2[1 : 1 + ROWS, 16 : 16 + COLS, :].reshape(ROWS * COLS, CH), 9 * CH)

    @pl.loop(0, 4)
    def _(k):
        r = k * 4
        g = conv_rows(d2, w2f[...], r, 4, 1) * s1[pl.ds(r + 2, 4)].reshape(4 * WIDE, CH)
        d1[pl.ds(r, 4)] = g.reshape(4, WIDE, CH)[:, 16 : 16 + COLS].astype(BF)

    weight_grad(t0, d1[...].reshape(ROWS * COLS, CH), 0)


def run_kernel(*args):
    vmem = pl.BlockSpec(memory_space=pltpu.VMEM)
    smem = pl.BlockSpec(memory_space=pltpu.SMEM)
    specs = [vmem] * 16
    specs[6] = smem
    specs[12] = smem
    dma = pltpu.SemaphoreType.DMA
    return pl.pallas_call(
        kernel,
        out_shape=(
            jax.ShapeDtypeStruct((18 * CH + 96, CH), F32),
            jax.ShapeDtypeStruct((8, 128), F32),
        ),
        in_specs=specs,
        out_specs=(vmem, vmem),
        scratch_shapes=[
            pltpu.VMEM((ROWS + 6, WIDE, CH), BF),
            pltpu.VMEM((ROWS + 6, WIDE, CH), BF),
            pltpu.VMEM((ROWS + 4, WIDE, CH), BF),
            pltpu.VMEM((ROWS + 2, WIDE, CH), BF),
            pltpu.VMEM((ROWS + 4, WIDE, CH), F32),
            pltpu.VMEM((ROWS + 2, WIDE, CH), F32),
            pltpu.VMEM((3 * CH, 3 * CH), BF),
            pltpu.VMEM((3 * CH, 3 * CH), BF),
            pltpu.VMEM((3 * CH, 3 * CH), BF),
            pltpu.VMEM((3, ROWS, COLS), F32),
            pltpu.VMEM((2, 3, ROWS, COLS), F32),
            pltpu.VMEM((384, PIX), BF),
            pltpu.VMEM((8, PIX), F32),
            pltpu.VMEM((8, PIX), F32),
            pltpu.VMEM((96, VW), F32),
            pltpu.VMEM((VW, 9 * VW), BF),
            pltpu.VMEM((VW, 9 * VW), BF),
            pltpu.VMEM((32, PIX + 256), BF),
            pltpu.VMEM((3, VW, PIX + 256), BF),
            pltpu.VMEM((3, VW, PIX + 256), BF),
            pltpu.VMEM((VW, PIX), F32),
            pltpu.VMEM((72, PIX + 256), F32),
            pltpu.VMEM((3, 3, 8, 128), F32),
            pltpu.VMEM((3, 3, 24, 128), F32),
            pltpu.VMEM((3, ROWS, COLS), BF),
            pltpu.VMEM((8, 3, ROWS, COLS), BF),
            pltpu.VMEM((ROWS + 4, 32, 256), F32),
            pltpu.VMEM((ROWS + 4, 32, 256), F32),
            pltpu.VMEM((ROWS + 2, WIDE, CH), BF),
            pltpu.VMEM((ROWS, COLS, CH), BF),
            pltpu.VMEM((3, CH, (ROWS + 2) * COLS), BF),
            pltpu.VMEM((3, CH, (ROWS + 2) * COLS), BF),
            pltpu.VMEM((1, 512), F32),
            pltpu.VMEM((3, 32, CH), F32),
            dma((8,)), dma((8,)), dma((2,)), dma((2,)), dma((2,)), dma((2,)), dma((8,)), dma((8,)),
        ],
        compiler_params=pltpu.CompilerParams(
            collective_id=0, has_side_effects=True, vmem_limit_bytes=56 * 1024 * 1024
        ),
    )(*args)


def per_device(
    features,
    conv_one_w,
    conv_one_b,
    conv_two_w,
    conv_two_b,
    out_conv_w,
    out_conv_b,
    vgg_one_w,
    vgg_one_b,
    vgg_two_w,
    vgg_two_b,
    lin_weights,
    row_lists,
    tap_index,
    tap_weight,
    target_tiles,
):
    grads, loss = run_kernel(
        features,
        conv_one_w,
        conv_one_b.reshape(1, CH),
        conv_two_w,
        conv_two_b.reshape(1, CH),
        jnp.transpose(out_conv_w, (0, 1, 3, 2)),
        out_conv_b,
        jnp.transpose(vgg_one_w, (1, 2, 3, 0)),
        vgg_one_b.reshape(1, VW),
        jnp.transpose(vgg_two_w, (2, 3, 0, 1)),
        vgg_two_b.reshape(1, VW),
        lin_weights.reshape(1, VW),
        row_lists,
        tap_index[0],
        tap_weight[0],
        target_tiles[0],
    )
    loss, grads = lax.psum((loss[0, 0], grads), ("lon", "grp"))
    grad_one = grads[: 9 * CH].reshape(3, 3, CH, CH)
    grad_two = grads[9 * CH : 18 * CH].reshape(3, 3, CH, CH)
    grad_out = grads[18 * CH :].reshape(3, 4, 8, CH)[:, :3, :3]
    return loss, grad_one, grad_two, jnp.transpose(grad_out, (0, 1, 3, 2))


def solution(mesh):
    in_specs = (
        P("grp", "lon", None),
        P(),
        P(),
        P(),
        P(),
        P(),
        P(),
        P(),
        P(),
        P(),
        P(),
        P(),
        P(("lon", "grp"), None, None),
        P(("lon", "grp"), None, None),
        P(("lon", "grp"), None, None),
        P(("lon", "grp"), None, None, None),
    )
    out_specs = (P(), P(), P(), P())
    return jax.shard_map(
        per_device, mesh=mesh, in_specs=in_specs, out_specs=out_specs, check_vma=False
    )
```

```python
import jax
import jax.numpy as jnp
from jax import lax
from jax.experimental import pallas as pl
from jax.experimental.pallas import tpu as pltpu
from jax.sharding import PartitionSpec as P

OFFSET = (-0.03, -0.088, -0.188)
SPREAD = (0.458, 0.448, 0.45)
LOSS_SCALE = 64.0

CH = 128
VW = 64
ROWS = 16
COLS = 128
WIDE = 160
TROWS = 64
PIX = TROWS * 128
BF = jnp.bfloat16
F32 = jnp.float32
MESH = pl.DeviceIdType.MESH

AROUND = ((-1, -1), (-1, 0), (-1, 1), (0, -1), (0, 1), (1, -1), (1, 0), (1, 1))


PARTS = ((0, (1, 2)), (1, (0, 2)), (2, (0, 1)))
GRAD_ROWS = 2496
PART = GRAD_ROWS // 3
SHARE = PART // 8
LINE_STEPS = [(d, k) for d in range(4) for k in range(2) if (d, k) != (0, 0)]
PLANE_STEPS = [(d, e) for d in range(4) for e in range(4) if (d, e) != (0, 0)]


def place():
    lon, grp = lax.axis_index("lon"), lax.axis_index("grp")
    return (lon // 8, (lon % 2) * 2 + grp // 2, (lon // 2) % 4), grp % 2


def device(xyz, core):
    x, y, z = xyz
    return ((x * 4 + z) * 2 + y // 2, (y % 2) * 2 + core)


def line_peers(axis):
    xyz, core = place()
    for d, k in LINE_STEPS:
        at, its_core = (xyz[axis] + d) % 4, (core + k) % 2
        peer = tuple(at if i == axis else xyz[i] for i in range(3))
        yield device(peer, its_core), at * 2 + its_core


def plane_peers(axes):
    xyz, core = place()
    u, v = axes
    for d, e in PLANE_STEPS:
        at_u, at_v = (xyz[u] + d) % 4, (xyz[v] + e) % 4
        peer = tuple(at_u if i == u else at_v if i == v else xyz[i] for i in range(3))
        yield device(peer, core), at_u * 4 + at_v


def sum_offsets():
    found = set()
    for axis, axes in PARTS:
        for d, k in LINE_STEPS:
            found.add(tuple(d if i == axis else 0 for i in range(3)) + (k,))
        for d, e in PLANE_STEPS:
            found.add(tuple(d if i == axes[0] else e if i == axes[1] else 0 for i in range(3)) + (0,))
    return sorted(found)


def rows8(start, size):
    return pl.ds(pl.multiple_of(start, 8), size)


def send(src, dst, send_sem, recv_sem, to):
    copy = pltpu.make_async_remote_copy(
        src_ref=src, dst_ref=dst, send_sem=send_sem, recv_sem=recv_sem, device_id=to, device_id_type=MESH
    )
    copy.start()
    return copy


def sum_all(grads, out, line_in, line_sum, plane_in, plane_sum, gathered, sems):
    ls, lr, ps, pr, gs, gr, os, orr = sems
    xyz, core = place()
    sent = []
    first = []
    for p, (axis, axes) in enumerate(PARTS):
        for i, (peer, index) in enumerate(line_peers(axis)):
            src = grads.at[rows8(p * PART + index * SHARE, SHARE)]
            first.append(send(src, line_in.at[p, i], ls.at[p, i], lr.at[p, i], peer))
    second = []
    for p, (axis, axes) in enumerate(PARTS):
        mine = xyz[axis] * 2 + core
        for copy in first[p * 7 : p * 7 + 7]:
            copy.wait()
        total = grads[rows8(p * PART + mine * SHARE, SHARE), :]
        for i in range(7):
            total = total + line_in[p, i]
        line_sum[p, 0:SHARE] = total
        for i, (peer, index) in enumerate(plane_peers(axes)):
            src = line_sum.at[p, rows8(index * 8, 8)]
            second.append(send(src, plane_in.at[p, i], ps.at[p, i], pr.at[p, i], peer))
    third = []
    for p, (axis, axes) in enumerate(PARTS):
        mine = xyz[axes[0]] * 4 + xyz[axes[1]]
        for copy in second[p * 15 : p * 15 + 15]:
            copy.wait()
        total = line_sum[p, rows8(mine * 8, 8), :]
        for i in range(15):
            total = total + plane_in[p, i]
        plane_sum[p] = total
        gathered[p, rows8(mine * 8, 8), :] = total
        for i, (peer, index) in enumerate(plane_peers(axes)):
            dst = gathered.at[p, rows8(mine * 8, 8)]
            third.append(send(plane_sum.at[p], dst, gs.at[p, i], gr.at[p, i], peer))
    fourth = []
    for p, (axis, axes) in enumerate(PARTS):
        mine = xyz[axis] * 2 + core
        at = rows8(p * PART + mine * SHARE, SHARE)
        for copy in third[p * 15 : p * 15 + 15]:
            copy.wait()
        for i, (peer, index) in enumerate(line_peers(axis)):
            fourth.append(send(gathered.at[p, 0:SHARE], out.at[at], os.at[p, i], orr.at[p, i], peer))
        out[at, :] = gathered[p, 0:SHARE]
    for copy in fourth:
        copy.wait()


def dot(a, b, ca=1, cb=0):
    return lax.dot_general(a, b, (((ca,), (cb,)), ((), ())), preferred_element_type=F32)


def span(start, size, unit):
    if isinstance(start, int):
        return pl.ds(start, size)
    return pl.ds(pl.multiple_of(start, unit), size)


def ext(delta, low, high):
    return low if delta < 0 else high


def conv_rows(src, weight, r, n, last=0):
    lhs = jnp.concatenate(
        [src[pl.ds(r + a, n)].reshape(n * WIDE, CH) for a in range(3)], axis=1
    )
    z = dot(lhs, weight, 1, last)
    return (
        pltpu.roll(z[:, :CH], 1, 0)
        + z[:, CH : 2 * CH]
        + pltpu.roll(z[:, 2 * CH :], n * WIDE - 1, 0)
    )


def act_slope(hidden):
    h = hidden.astype(F32)
    s = jax.nn.sigmoid(h)
    return (h * s).astype(BF), s * (1.0 + h * (1.0 - s))


def lane_masks(n):
    col = lax.broadcasted_iota(jnp.int32, (1, 128), 1)
    return col > 0, col < 127


def shift_store(ref, y, row0, n):
    first, last = lane_masks(n)
    for r in range(n):
        part = y[:, r * 128 : (r + 1) * 128]
        at = span((row0 + r + 1) * 128, 128, 128)
        ref[0, :, at] = jnp.where(first, pltpu.roll(part, 1, 1), 0.0).astype(BF)
        ref[1, :, at] = part.astype(BF)
        ref[2, :, at] = jnp.where(last, pltpu.roll(part, 127, 1), 0.0).astype(BF)


def per_channel(values):
    row = lax.broadcasted_iota(jnp.int32, (8, 1), 0)
    out = jnp.full((8, 1), values[2], F32)
    out = jnp.where(row == 0, values[0], out)
    return jnp.where(row == 1, values[1], out)


def store_scaled(zs, colours, row0, n):
    row = lax.broadcasted_iota(jnp.int32, (8, 1), 0)
    z = jnp.where(row < 3, (colours - per_channel(OFFSET)) / per_channel(SPREAD), 0.0)
    first, last = lane_masks(n)
    for r in range(n):
        part = z[:, r * 128 : (r + 1) * 128]
        stack = jnp.concatenate(
            [
                jnp.where(first, pltpu.roll(part, 1, 1), 0.0),
                part,
                jnp.where(last, pltpu.roll(part, 127, 1), 0.0),
                jnp.zeros_like(part),
            ],
            axis=0,
        )
        zs[:, span((row0 + r + 1) * 128, 128, 128)] = stack.astype(BF)


def vgg_first(zs, fs, v1, v1b, n):
    @pl.loop(0, TROWS // n)
    def _(k):
        r0 = k * n
        rhs = jnp.concatenate(
            [zs[:, span((r0 + a) * 128, n * 128, 128)] for a in range(3)], axis=0
        )
        y = jnp.maximum(dot(v1, rhs) + v1b, 0.0)
        shift_store(fs, y, r0, n)


def nine_taps(ref, r0, n):
    return jnp.concatenate(
        [ref[b, :, span((r0 + a) * 128, n * 128, 128)] for a in range(3) for b in range(3)], axis=0
    )


def inv_norm(f):
    return lax.rsqrt(jnp.sum(f * f, axis=0, keepdims=True) + 1e-05)


def kernel(
    feat, w1, b1, w2, b2, wo, bo, v1w, v1b, v2w, v2b, lin, rows_ref, tap_i, tap_w, target,
    one_out, two_out, rest_out,
    f_ref, a0, a1, a2, s1, s2, w1c, w2c, w2f, c_own, c_near, hot, al, ar, v1f, v2c, v2t,
    zs, fs, gs, unit_t, y_ref, tb, pb, ca, ca_near, own_e, all_e, d2, d1, t0, t1, loss_acc, wof,
    grads, total, line_in, line_sum, plane_in, plane_sum, gathered,
    halo_send, halo_recv, col_send, col_recv, tab_send, tab_recv, adj_send, adj_recv, out_sem,
    *sum_sems,
):
    lon, grp = lax.axis_index("lon"), lax.axis_index("grp")
    n_lon, n_grp = lax.axis_size("lon"), lax.axis_size("grp")

    def near(dl, dg):
        return (lax.rem(lon + dl + n_lon, n_lon), lax.rem(grp + dg + n_grp, n_grp))

    barrier = pltpu.get_barrier_semaphore()
    for dl, dg in AROUND:
        pl.semaphore_signal(barrier, inc=1, device_id=near(dl, dg), device_id_type=MESH)
    xyz, core = place()
    peers = sum_offsets()
    for off in peers:
        peer = device([(xyz[i] + off[i]) % 4 for i in range(3)], (core + off[3]) % 2)
        pl.semaphore_signal(barrier, inc=1, device_id=peer, device_id_type=MESH)

    for a in range(3):
        for b in range(3):
            rows, cols = slice(a * CH, (a + 1) * CH), slice(b * CH, (b + 1) * CH)
            w1c[rows, cols] = w1[a, b]
            w2c[rows, cols] = w2[a, b]
            w2f[cols, rows] = w2[2 - a, 2 - b]
    v1f[...] = jnp.zeros_like(v1f)
    wof[...] = jnp.zeros_like(wof)
    for a in range(3):
        for b in range(3):
            for c in range(3):
                v1f[a * 32 + b * 8 + c : a * 32 + b * 8 + c + 1, :] = v1w[c, a, b : b + 1].astype(F32)
            wof[a, b * 8 : b * 8 + 3, :] = wo[a, b].astype(F32)
            v2c[:, (a * 3 + b) * VW : (a * 3 + b + 1) * VW] = v2w[a, b]
            v2t[:, (a * 3 + b) * VW : (a * 3 + b + 1) * VW] = (
                v2w[2 - a, 2 - b].astype(F32).T.astype(BF)
            )
    v1 = v1f[...].T.astype(BF)
    v1b_col = v1b[...].reshape(VW, 1)
    v2b_col = v2b[...].reshape(VW, 1)
    lin_col = lin[...].reshape(VW, 1)

    zs[:, 0:128] = jnp.zeros((32, 128), BF)
    zs[:, PIX + 128 :] = jnp.zeros((32, 128), BF)
    for ref in (fs, gs):
        ref[:, :, 0:128] = jnp.zeros((3, VW, 128), BF)
        ref[:, :, PIX + 128 :] = jnp.zeros((3, VW, 128), BF)
    y_ref[:, 0:128] = jnp.zeros((72, 128), F32)
    y_ref[:, PIX + 128 :] = jnp.zeros((72, 128), F32)
    pb[:, :, 0:8, :] = jnp.zeros((3, 3, 8, 128), F32)
    pb[:, :, 16:24, :] = jnp.zeros((3, 3, 8, 128), F32)
    own_e[...] = jnp.zeros_like(own_e)
    all_e[...] = jnp.zeros_like(all_e)

    pl.semaphore_wait(barrier, len(AROUND) + len(peers))
    take_r = {-1: pl.ds(0, 3), 0: pl.ds(0, ROWS), 1: pl.ds(ROWS - 3, 3)}
    take_c = {-1: pl.ds(0, 16), 0: pl.ds(0, COLS), 1: pl.ds(COLS - 16, 16)}
    land_r = {-1: pl.ds(ROWS + 3, 3), 0: pl.ds(3, ROWS), 1: pl.ds(0, 3)}
    land_c = {-1: pl.ds(COLS + 16, 16), 0: pl.ds(16, COLS), 1: pl.ds(0, 16)}
    halo = []
    for i, (dl, dg) in enumerate(AROUND):
        copy = pltpu.make_async_remote_copy(
            src_ref=feat.at[take_r[dg], take_c[dl]],
            dst_ref=f_ref.at[land_r[dg], land_c[dl]],
            send_sem=halo_send.at[i],
            recv_sem=halo_recv.at[i],
            device_id=near(dl, dg),
            device_id_type=MESH,
        )
        copy.start()
        halo.append(copy)
    f_ref[3 : 3 + ROWS, 16 : 16 + COLS, :] = feat[...]

    for r in range(TROWS):
        tgt = target[:, r, :].astype(F32)
        unit_t[0:8, r * 128 : (r + 1) * 128] = jnp.concatenate(
            [tgt, jnp.zeros((5, 128), F32)], axis=0
        )

    @pl.loop(0, 8)
    def _(k):
        store_scaled(zs, unit_t[0:8, span(k * 1024, 1024, 128)], k * 8, 8)

    vgg_first(zs, fs, v1, v1b_col, 4)

    @pl.loop(0, TROWS // 4)
    def _(k):
        f = jnp.maximum(dot(v2c[...], nine_taps(fs, k * 4, 4)) + v2b_col, 0.0)
        unit_t[:, span(k * 512, 512, 128)] = f * inv_norm(f)

    @pl.loop(0, 8)
    def _(k):
        at = span(k * 1024, 1024, 128)
        index = tap_i[:, at]
        weight = tap_w[:, at]
        column = lax.shift_left(lax.shift_right_logical(index, 10), 7) + jnp.bitwise_and(index, 127)
        slot = jnp.bitwise_and(lax.shift_right_logical(index, 7), 7)
        left = jnp.min(column, axis=0, keepdims=True)
        top = jnp.min(slot, axis=0, keepdims=True)
        is_left, is_top = column == left, slot == top

        def corner(cond):
            return jnp.sum(jnp.where(cond, weight, 0.0), axis=0, keepdims=True)

        not_left, not_top = jnp.logical_not(is_left), jnp.logical_not(is_top)
        w_tl, w_tr = corner(is_top & is_left), corner(is_top & not_left)
        w_bl, w_br = corner(not_top & is_left), corner(not_top & not_left)
        j = lax.broadcasted_iota(jnp.int32, (8, 1024), 0)
        on_top, on_next = j == top, j == top + 1
        al[:, at] = jnp.where(on_top, w_tl, jnp.where(on_next, w_bl, 0.0))
        ar[:, at] = jnp.where(on_top, w_tr, jnp.where(on_next, w_br, 0.0))
        x = lax.broadcasted_iota(jnp.int32, (384, 1024), 0)
        hot[:, at] = jnp.where(x == left, 1.0, 0.0).astype(BF)

    for copy in halo:
        copy.wait()
    north, south = grp == 0, grp == n_grp - 1

    @pl.loop(0, ROWS + 6)
    def _(r):
        a0[r] = act_slope(f_ref[r])[0]

    def clear(ref, rows):
        @pl.when(north)
        def _():
            ref[0:rows] = jnp.zeros((rows, WIDE, CH), BF)

        @pl.when(south)
        def _():
            ref[ref.shape[0] - rows :] = jnp.zeros((rows, WIDE, CH), BF)

    clear(a0, 3)

    @pl.loop(0, 5)
    def _(k):
        r = k * 4
        h = (conv_rows(a0, w1c[...], r, 4) + b1[...]).astype(BF)
        act, slope = act_slope(h)
        a1[pl.ds(r, 4)] = act.reshape(4, WIDE, CH)
        s1[pl.ds(r, 4)] = slope.reshape(4, WIDE, CH)

    clear(a1, 2)

    @pl.loop(0, 6)
    def _(k):
        r = k * 3
        f = f_ref[pl.ds(r + 2, 3)].reshape(3 * WIDE, CH).astype(F32)
        h = (f + conv_rows(a1, w2c[...], r, 3) + b2[...]).astype(BF)
        act, slope = act_slope(h)
        a2[pl.ds(r, 3)] = act.reshape(3, WIDE, CH)
        s2[pl.ds(r, 3)] = slope.reshape(3, WIDE, CH)

    clear(a2, 1)

    wo_cat = jnp.concatenate([wof[a] for a in range(3)], axis=1).astype(BF)
    for r in range(ROWS):
        rhs = jnp.concatenate([a2[r + a] for a in range(3)], axis=1)
        z = dot(wo_cat, rhs, 1, 1)
        colour = z[0:8, 15 : 15 + COLS] + z[8:16, 16 : 16 + COLS] + z[16:24, 17 : 17 + COLS]
        for c in range(3):
            c_own[c, r : r + 1, :] = colour[c : c + 1] + bo[c]

    colours = []
    for i, dl in enumerate((-1, 1)):
        copy = pltpu.make_async_remote_copy(
            src_ref=c_own,
            dst_ref=c_near.at[1 - i],
            send_sem=col_send.at[i],
            recv_sem=col_recv.at[1 - i],
            device_id=near(dl, 0),
            device_id_type=MESH,
        )
        copy.start()
        colours.append(copy)

    for act, turned, first_row in ((a0, t0, 2), (a1, t1, 1)):

        @pl.loop(0, ROWS + 2)
        def _(r, act=act, turned=turned, first_row=first_row):
            block = act[r + first_row].astype(F32).T
            at = span(r * 128, 128, 128)
            for b in range(3):
                turned[b, :, at] = block[:, 15 + b : 15 + b + COLS].astype(BF)

    for copy in colours:
        copy.wait()

    start = rows_ref[1, 0, 0]
    slabs = (c_near.at[0], c_own, c_near.at[1])
    table = jnp.concatenate(
        [
            jnp.concatenate([slab[c, pl.ds(start, 8), :] for c in range(3)], axis=0)
            for slab in slabs
        ],
        axis=1,
    )
    table = jnp.concatenate([table, pltpu.roll(table, 383, 1)], axis=0)
    table_hi = table.astype(BF)
    table_lo = (table - table_hi.astype(F32)).astype(BF)
    table = jnp.concatenate([table_hi, table_lo], axis=0)

    @pl.loop(0, 8)
    def _(k):
        at = span(k * 1024, 1024, 128)
        got = dot(table, hot[:, at])
        got = got[0:48] + got[48:96]
        w_left, w_right = al[:, at], ar[:, at]
        picture = [
            jnp.sum(
                got[c * 8 : c * 8 + 8] * w_left + got[24 + c * 8 : 32 + c * 8] * w_right,
                axis=0,
                keepdims=True,
            )
            for c in range(3)
        ]
        picture = jnp.concatenate(picture + [jnp.zeros((5, 1024), F32)], axis=0)
        store_scaled(zs, picture, k * 8, 8)

    vgg_first(zs, fs, v1, v1b_col, 4)
    loss_acc[...] = jnp.zeros_like(loss_acc)

    @pl.loop(0, TROWS // 4)
    def _(k):
        f = jnp.maximum(dot(v2c[...], nine_taps(fs, k * 4, 4)) + v2b_col, 0.0)
        inv = inv_norm(f)
        u = f * inv
        diff = u - unit_t[:, span(k * 512, 512, 128)]
        weighted = lin_col * diff
        loss_acc[...] += jnp.sum(weighted * diff, axis=0, keepdims=True)
        g = weighted * (2.0 * LOSS_SCALE / PIX)
        g = inv * (g - u * jnp.sum(g * u, axis=0, keepdims=True))
        shift_store(gs, jnp.where(f > 0.0, g, 0.0), k * 4, 4)

    loss = jnp.sum(loss_acc[...], axis=1, keepdims=True) * (1.0 / PIX)
    grads[18 * CH + 96 : 18 * CH + 104, :] = jnp.broadcast_to(loss, (8, 128))
    grads[18 * CH + 104 :, :] = jnp.zeros((GRAD_ROWS - 18 * CH - 104, CH), F32)
    for p in range(3):
        line_sum[p, SHARE:] = jnp.zeros((128 - SHARE, CH), F32)

    v1_back = jnp.concatenate(
        [
            v1f[(2 - a) * 32 + (2 - b) * 8 : (2 - a) * 32 + (2 - b) * 8 + 8, :]
            for b in range(3)
            for a in range(3)
        ],
        axis=0,
    ).astype(BF)

    @pl.loop(0, TROWS // 4)
    def _(k):
        g = dot(v2t[...], nine_taps(gs, k * 4, 4)).astype(BF)
        at = span((k * 4 + 1) * 128, 512, 128)
        g = jnp.where(fs[1, :, at] > 0, g, jnp.zeros_like(g))
        y_ref[:, at] = dot(v1_back, g)

    def table_adjoint(k, acc):
        at = span(k * 1024, 1024, 128)
        part = []
        for b in range(3):
            part.append(
                sum(
                    y_ref[(b * 3 + a) * 8 : (b * 3 + a) * 8 + 8, span((k * 8 + a) * 128, 1024, 128)]
                    for a in range(3)
                )
            )
        col = jnp.bitwise_and(lax.broadcasted_iota(jnp.int32, (8, 1024), 1), 127)
        dz = (
            jnp.where(col > 0, pltpu.roll(part[0], 1, 1), 0.0)
            + part[1]
            + jnp.where(col < 127, pltpu.roll(part[2], 1023, 1), 0.0)
        )
        dz = dz.astype(BF).astype(F32) / per_channel(SPREAD)
        spread = jnp.concatenate(
            [w[:, at] * dz[c : c + 1] for w in (al, ar) for c in range(3)], axis=0
        )
        hi = spread.astype(BF)
        lo = (spread - hi.astype(F32)).astype(BF)
        return acc + dot(jnp.concatenate([hi, lo], axis=0), hot[:, at], 1, 1)

    acc = lax.fori_loop(0, 8, table_adjoint, jnp.zeros((96, 384), F32))
    acc = acc[0:48] + acc[48:96]
    adjoint = acc[0:24] + pltpu.roll(acc[24:48], 1, 1)
    for k in range(3):
        for c in range(3):
            tb[k, c] = adjoint[c * 8 : c * 8 + 8, k * 128 : (k + 1) * 128]
    pb[1, :, 8:16, :] = tb[1]

    returned = []
    for i, (k, dl) in enumerate(((0, -1), (2, 1))):
        copy = pltpu.make_async_remote_copy(
            src_ref=tb.at[k],
            dst_ref=pb.at[k, :, pl.ds(8, 8), :],
            send_sem=tab_send.at[i],
            recv_sem=tab_recv.at[i],
            device_id=near(dl, 0),
            device_id_type=MESH,
        )
        copy.start()
        returned.append(copy)
    for copy in returned:
        copy.wait()

    for c in range(3):
        placed = sum(pb[k, c, pl.ds(8 - rows_ref[k, 0, 0], ROWS), :] for k in range(3))
        ca[c] = placed.astype(BF)

    exchanged = []
    for i, (dl, dg) in enumerate(AROUND):
        copy = pltpu.make_async_remote_copy(
            src_ref=ca,
            dst_ref=ca_near.at[7 - i],
            send_sem=adj_send.at[i],
            recv_sem=adj_recv.at[7 - i],
            device_id=near(dl, dg),
            device_id_type=MESH,
        )
        copy.start()
        exchanged.append(copy)

    def taps_of(target_e, c, field):
        for b in range(3):
            moved = pltpu.roll(field, 384 - (111 + 2 - b), 1)[:, 0:256]
            target_e[:, b * 8 + c, :] = moved

    def patches(source_e, r):
        return jnp.concatenate([source_e[r + a] for a in range(3)], axis=0)[:, :WIDE].astype(BF)

    rows2 = jnp.zeros((2, 384), F32)
    own = [ca[c].astype(F32) for c in range(3)]
    for c in range(3):
        side = jnp.zeros((ROWS, 128), F32)
        middle = jnp.concatenate([side, own[c], side], axis=1)
        taps_of(own_e, c, jnp.concatenate([rows2, middle, rows2], axis=0))
    grad_out = jnp.zeros((96, CH), F32)
    for r in range(ROWS + 2):
        grad_out += dot(patches(own_e, r), a2[r])
    for a in range(3):
        base = 18 * CH + (2 - a) * 32
        grads[base : base + 32, :] = grad_out[a * 32 : a * 32 + 32]

    for copy in exchanged:
        copy.wait()
    at_of = {delta: i for i, delta in enumerate(AROUND)}
    has_north = jnp.where(north, 0.0, 1.0)
    has_south = jnp.where(south, 0.0, 1.0)
    for c in range(3):

        def line(dg):
            parts = [
                own[c] if (dl, dg) == (0, 0) else ca_near[at_of[(dl, dg)], c].astype(F32)
                for dl in (-1, 0, 1)
            ]
            return jnp.concatenate(parts, axis=1)

        field = jnp.concatenate(
            [line(-1)[ROWS - 2 :] * has_north, line(0), line(1)[0:2] * has_south], axis=0
        )
        taps_of(all_e, c, field)

    wo_flip = jnp.concatenate([wof[2 - a] for a in range(3)], axis=0).astype(BF)
    for r in range(ROWS + 2):
        d2[r] = (dot(patches(all_e, r), wo_flip, 0, 0) * s2[r]).astype(BF)
    clear(d2, 1)

    def weight_grad(turned, adj, base):
        for a in range(3):
            for b in range(3):
                at = base + (a * 3 + b) * CH
                grads[at : at + CH, :] = dot(turned[b, :, a * 128 : a * 128 + ROWS * 128], adj)

    weight_grad(t1, d2[1 : 1 + ROWS, 16 : 16 + COLS, :].reshape(ROWS * COLS, CH), 9 * CH)

    @pl.loop(0, 4)
    def _(k):
        r = k * 4
        g = conv_rows(d2, w2f[...], r, 4, 1) * s1[pl.ds(r + 2, 4)].reshape(4 * WIDE, CH)
        d1[pl.ds(r, 4)] = g.reshape(4, WIDE, CH)[:, 16 : 16 + COLS].astype(BF)

    weight_grad(t0, d1[...].reshape(ROWS * COLS, CH), 0)

    sum_all(grads, total, line_in, line_sum, plane_in, plane_sum, gathered, sum_sems)
    outs = []
    for i, (out, at, size) in enumerate(
        ((one_out, 0, 9 * CH), (two_out, 9 * CH, 9 * CH), (rest_out, 18 * CH, 104))
    ):
        copy = pltpu.make_async_copy(total.at[at : at + size], out, out_sem.at[i])
        copy.start()
        outs.append(copy)
    for copy in outs:
        copy.wait()


def run_kernel(*args):
    vmem = pl.BlockSpec(memory_space=pltpu.VMEM)
    smem = pl.BlockSpec(memory_space=pltpu.SMEM)
    specs = [vmem] * 16
    specs[6] = smem
    specs[12] = smem
    dma = pltpu.SemaphoreType.DMA
    return pl.pallas_call(
        kernel,
        out_shape=(
            jax.ShapeDtypeStruct((9 * CH, CH), F32),
            jax.ShapeDtypeStruct((9 * CH, CH), F32),
            jax.ShapeDtypeStruct((104, CH), F32),
        ),
        in_specs=specs,
        out_specs=(pl.BlockSpec(memory_space=pl.ANY),) * 3,
        scratch_shapes=[
            pltpu.VMEM((ROWS + 6, WIDE, CH), BF),
            pltpu.VMEM((ROWS + 6, WIDE, CH), BF),
            pltpu.VMEM((ROWS + 4, WIDE, CH), BF),
            pltpu.VMEM((ROWS + 2, WIDE, CH), BF),
            pltpu.VMEM((ROWS + 4, WIDE, CH), F32),
            pltpu.VMEM((ROWS + 2, WIDE, CH), F32),
            pltpu.VMEM((3 * CH, 3 * CH), BF),
            pltpu.VMEM((3 * CH, 3 * CH), BF),
            pltpu.VMEM((3 * CH, 3 * CH), BF),
            pltpu.VMEM((3, ROWS, COLS), F32),
            pltpu.VMEM((2, 3, ROWS, COLS), F32),
            pltpu.VMEM((384, PIX), BF),
            pltpu.VMEM((8, PIX), F32),
            pltpu.VMEM((8, PIX), F32),
            pltpu.VMEM((96, VW), F32),
            pltpu.VMEM((VW, 9 * VW), BF),
            pltpu.VMEM((VW, 9 * VW), BF),
            pltpu.VMEM((32, PIX + 256), BF),
            pltpu.VMEM((3, VW, PIX + 256), BF),
            pltpu.VMEM((3, VW, PIX + 256), BF),
            pltpu.VMEM((VW, PIX), F32),
            pltpu.VMEM((72, PIX + 256), F32),
            pltpu.VMEM((3, 3, 8, 128), F32),
            pltpu.VMEM((3, 3, 24, 128), F32),
            pltpu.VMEM((3, ROWS, COLS), BF),
            pltpu.VMEM((8, 3, ROWS, COLS), BF),
            pltpu.VMEM((ROWS + 4, 32, 256), F32),
            pltpu.VMEM((ROWS + 4, 32, 256), F32),
            pltpu.VMEM((ROWS + 2, WIDE, CH), BF),
            pltpu.VMEM((ROWS, COLS, CH), BF),
            pltpu.VMEM((3, CH, (ROWS + 2) * COLS), BF),
            pltpu.VMEM((3, CH, (ROWS + 2) * COLS), BF),
            pltpu.VMEM((1, 512), F32),
            pltpu.VMEM((3, 32, CH), F32),
            pltpu.VMEM((GRAD_ROWS, CH), F32),
            pltpu.VMEM((GRAD_ROWS, CH), F32),
            pltpu.VMEM((3, 7, SHARE, CH), F32),
            pltpu.VMEM((3, 128, CH), F32),
            pltpu.VMEM((3, 15, 8, CH), F32),
            pltpu.VMEM((3, 8, CH), F32),
            pltpu.VMEM((3, 128, CH), F32),
            dma((8,)), dma((8,)), dma((2,)), dma((2,)), dma((2,)), dma((2,)), dma((8,)), dma((8,)), dma((3,)),
            dma((3, 7)), dma((3, 7)), dma((3, 15)), dma((3, 15)),
            dma((3, 15)), dma((3, 15)), dma((3, 7)), dma((3, 7)),
        ],
        compiler_params=pltpu.CompilerParams(
            collective_id=0, has_side_effects=True, vmem_limit_bytes=56 * 1024 * 1024
        ),
    )(*args)


def per_device(
    features,
    conv_one_w,
    conv_one_b,
    conv_two_w,
    conv_two_b,
    out_conv_w,
    out_conv_b,
    vgg_one_w,
    vgg_one_b,
    vgg_two_w,
    vgg_two_b,
    lin_weights,
    row_lists,
    tap_index,
    tap_weight,
    target_tiles,
):
    grad_one, grad_two, rest = run_kernel(
        features,
        conv_one_w,
        conv_one_b.reshape(1, CH),
        conv_two_w,
        conv_two_b.reshape(1, CH),
        jnp.transpose(out_conv_w, (0, 1, 3, 2)),
        out_conv_b,
        jnp.transpose(vgg_one_w, (1, 2, 3, 0)),
        vgg_one_b.reshape(1, VW),
        jnp.transpose(vgg_two_w, (2, 3, 0, 1)),
        vgg_two_b.reshape(1, VW),
        lin_weights.reshape(1, VW),
        jnp.transpose(row_lists, (1, 0, 2)),
        tap_index[0],
        tap_weight[0],
        target_tiles[0],
    )
    grad_out = rest[:96].reshape(3, 4, 8, CH)[:, :3, :3]
    return (
        rest[96, 0],
        grad_one.reshape(3, 3, CH, CH),
        grad_two.reshape(3, 3, CH, CH),
        jnp.transpose(grad_out, (0, 1, 3, 2)),
    )


def solution(mesh):
    in_specs = (
        P("grp", "lon", None),
        P(),
        P(),
        P(),
        P(),
        P(),
        P(),
        P(),
        P(),
        P(),
        P(),
        P(),
        P(("lon", "grp"), None, None),
        P(("lon", "grp"), None, None),
        P(("lon", "grp"), None, None),
        P(("lon", "grp"), None, None, None),
    )
    out_specs = (P(), P(), P(), P())
    return jax.shard_map(
        per_device, mesh=mesh, in_specs=in_specs, out_specs=out_specs, check_vma=False
    )
```

```python
import jax
import jax.numpy as jnp
from jax import lax
from jax.experimental import pallas as pl
from jax.experimental.pallas import tpu as pltpu
from jax.sharding import PartitionSpec as P

OFFSET = (-0.03, -0.088, -0.188)
SPREAD = (0.458, 0.448, 0.45)
LOSS_SCALE = 64.0

CH = 128
VW = 64
ROWS = 16
COLS = 128
WIDE = 160
TROWS = 64
PIX = TROWS * 128
BF = jnp.bfloat16
F32 = jnp.float32
MESH = pl.DeviceIdType.MESH

AROUND = ((-1, -1), (-1, 0), (-1, 1), (0, -1), (0, 1), (1, -1), (1, 0), (1, 1))


PARTS = ((0, (1, 2)), (1, (0, 2)), (2, (0, 1)))
GRAD_ROWS = 2496
REST = 9 * CH
ONE = 9 * CH + 104
PART = GRAD_ROWS // 3
SHARE = PART // 8
LINE_STEPS = [(d, k) for d in range(4) for k in range(2) if (d, k) != (0, 0)]
PLANE_STEPS = [(d, e) for d in range(4) for e in range(4) if (d, e) != (0, 0)]


def place():
    lon, grp = lax.axis_index("lon"), lax.axis_index("grp")
    return (lon // 8, (lon % 2) * 2 + grp // 2, (lon // 2) % 4), grp % 2


def device(xyz, core):
    x, y, z = xyz
    return ((x * 4 + z) * 2 + y // 2, (y % 2) * 2 + core)


def line_peers(axis):
    xyz, core = place()
    for d, k in LINE_STEPS:
        at, its_core = (xyz[axis] + d) % 4, (core + k) % 2
        peer = tuple(at if i == axis else xyz[i] for i in range(3))
        yield device(peer, its_core), at * 2 + its_core


def plane_peers(axes):
    xyz, core = place()
    u, v = axes
    for d, e in PLANE_STEPS:
        at_u, at_v = (xyz[u] + d) % 4, (xyz[v] + e) % 4
        peer = tuple(at_u if i == u else at_v if i == v else xyz[i] for i in range(3))
        yield device(peer, core), at_u * 4 + at_v


def sum_offsets():
    found = set()
    for axis, axes in PARTS:
        for d, k in LINE_STEPS:
            found.add(tuple(d if i == axis else 0 for i in range(3)) + (k,))
        for d, e in PLANE_STEPS:
            found.add(tuple(d if i == axes[0] else e if i == axes[1] else 0 for i in range(3)) + (0,))
    return sorted(found)


def rows8(start, size):
    return pl.ds(pl.multiple_of(start, 8), size)


def send(src, dst, send_sem, recv_sem, to):
    copy = pltpu.make_async_remote_copy(
        src_ref=src, dst_ref=dst, send_sem=send_sem, recv_sem=recv_sem, device_id=to, device_id_type=MESH
    )
    copy.start()
    return copy


def scatter_part(p, grads, line_in, sems):
    copies = []
    for i, (peer, index) in enumerate(line_peers(PARTS[p][0])):
        src = grads.at[rows8(p * PART + index * SHARE, SHARE)]
        copies.append(send(src, line_in.at[p, i], sems[0].at[p, i], sems[1].at[p, i], peer))
    return copies


def sum_all(first, grads, out, line_in, line_sum, plane_in, plane_sum, gathered, sems):
    ls, lr, ps, pr, gs, gr, os, orr = sems
    xyz, core = place()
    second = []
    for p, (axis, axes) in enumerate(PARTS):
        mine = xyz[axis] * 2 + core
        for copy in first[p * 7 : p * 7 + 7]:
            copy.wait()
        total = grads[rows8(p * PART + mine * SHARE, SHARE), :]
        for i in range(7):
            total = total + line_in[p, i]
        line_sum[p, 0:SHARE] = total
        for i, (peer, index) in enumerate(plane_peers(axes)):
            src = line_sum.at[p, rows8(index * 8, 8)]
            second.append(send(src, plane_in.at[p, i], ps.at[p, i], pr.at[p, i], peer))
    third = []
    for p, (axis, axes) in enumerate(PARTS):
        mine = xyz[axes[0]] * 4 + xyz[axes[1]]
        for copy in second[p * 15 : p * 15 + 15]:
            copy.wait()
        total = line_sum[p, rows8(mine * 8, 8), :]
        for i in range(15):
            total = total + plane_in[p, i]
        plane_sum[p] = total
        gathered[p, rows8(mine * 8, 8), :] = total
        for i, (peer, index) in enumerate(plane_peers(axes)):
            dst = gathered.at[p, rows8(mine * 8, 8)]
            third.append(send(plane_sum.at[p], dst, gs.at[p, i], gr.at[p, i], peer))
    fourth = []
    for p, (axis, axes) in enumerate(PARTS):
        mine = xyz[axis] * 2 + core
        at = rows8(p * PART + mine * SHARE, SHARE)
        for copy in third[p * 15 : p * 15 + 15]:
            copy.wait()
        for i, (peer, index) in enumerate(line_peers(axis)):
            fourth.append(send(gathered.at[p, 0:SHARE], out.at[at], os.at[p, i], orr.at[p, i], peer))
        out[at, :] = gathered[p, 0:SHARE]
    for copy in fourth:
        copy.wait()


def dot(a, b, ca=1, cb=0):
    return lax.dot_general(a, b, (((ca,), (cb,)), ((), ())), preferred_element_type=F32)


def span(start, size, unit):
    if isinstance(start, int):
        return pl.ds(start, size)
    return pl.ds(pl.multiple_of(start, unit), size)


def ext(delta, low, high):
    return low if delta < 0 else high


def conv_rows(src, weight, r, n, last=0):
    lhs = jnp.concatenate(
        [src[pl.ds(r + a, n)].reshape(n * WIDE, CH) for a in range(3)], axis=1
    )
    z = dot(lhs, weight, 1, last)
    return (
        pltpu.roll(z[:, :CH], 1, 0)
        + z[:, CH : 2 * CH]
        + pltpu.roll(z[:, 2 * CH :], n * WIDE - 1, 0)
    )


def act_slope(hidden):
    h = hidden.astype(F32)
    s = jax.nn.sigmoid(h)
    return (h * s).astype(BF), s * (1.0 + h * (1.0 - s))


def lane_masks(n):
    col = lax.broadcasted_iota(jnp.int32, (1, 128), 1)
    return col > 0, col < 127


def shift_store(ref, y, row0, n):
    first, last = lane_masks(n)
    for r in range(n):
        part = y[:, r * 128 : (r + 1) * 128]
        at = span((row0 + r + 1) * 128, 128, 128)
        ref[0, :, at] = jnp.where(first, pltpu.roll(part, 1, 1), 0.0).astype(BF)
        ref[1, :, at] = part.astype(BF)
        ref[2, :, at] = jnp.where(last, pltpu.roll(part, 127, 1), 0.0).astype(BF)


def per_channel(values):
    row = lax.broadcasted_iota(jnp.int32, (8, 1), 0)
    out = jnp.full((8, 1), values[2], F32)
    out = jnp.where(row == 0, values[0], out)
    return jnp.where(row == 1, values[1], out)


def store_scaled(zs, colours, row0, n):
    row = lax.broadcasted_iota(jnp.int32, (8, 1), 0)
    z = jnp.where(row < 3, (colours - per_channel(OFFSET)) / per_channel(SPREAD), 0.0)
    first, last = lane_masks(n)
    for r in range(n):
        part = z[:, r * 128 : (r + 1) * 128]
        stack = jnp.concatenate(
            [
                jnp.where(first, pltpu.roll(part, 1, 1), 0.0),
                part,
                jnp.where(last, pltpu.roll(part, 127, 1), 0.0),
                jnp.zeros_like(part),
            ],
            axis=0,
        )
        zs[:, span((row0 + r + 1) * 128, 128, 128)] = stack.astype(BF)


def vgg_first(zs, fs, v1, v1b, n):
    @pl.loop(0, TROWS // n, unroll=4)
    def _(k):
        r0 = k * n
        rhs = jnp.concatenate(
            [zs[:, span((r0 + a) * 128, n * 128, 128)] for a in range(3)], axis=0
        )
        y = jnp.maximum(dot(v1, rhs) + v1b, 0.0)
        shift_store(fs, y, r0, n)


def nine_taps(ref, r0, n):
    return jnp.concatenate(
        [ref[b, :, span((r0 + a) * 128, n * 128, 128)] for a in range(3) for b in range(3)], axis=0
    )


def inv_norm(f):
    return lax.rsqrt(jnp.sum(f * f, axis=0, keepdims=True) + 1e-05)


def kernel(
    feat, w1, b1, w2, b2, wo, bo, v1w, v1b, v2w, v2b, lin, rows_ref, tap_i, tap_w, target,
    one_out, two_out, rest_out,
    f_ref, a0, a1, a2, s1, s2, w1c, w2c, w2f, c_own, c_near, hot, al, ar, v1f, v2c, v2t,
    zs, fs, gs, unit_t, y_ref, tb, pb, ca, ca_near, own_e, all_e, d2, d1, t0, t1, loss_acc, wof,
    grads, total, line_in, line_sum, plane_in, plane_sum, gathered,
    halo_send, halo_recv, col_send, col_recv, tab_send, tab_recv, adj_send, adj_recv, out_sem,
    *sum_sems,
):
    lon, grp = lax.axis_index("lon"), lax.axis_index("grp")
    n_lon, n_grp = lax.axis_size("lon"), lax.axis_size("grp")

    def near(dl, dg):
        return (lax.rem(lon + dl + n_lon, n_lon), lax.rem(grp + dg + n_grp, n_grp))

    barrier = pltpu.get_barrier_semaphore()
    for dl, dg in AROUND:
        pl.semaphore_signal(barrier, inc=1, device_id=near(dl, dg), device_id_type=MESH)
    xyz, core = place()
    peers = sum_offsets()
    for off in peers:
        peer = device([(xyz[i] + off[i]) % 4 for i in range(3)], (core + off[3]) % 2)
        pl.semaphore_signal(barrier, inc=1, device_id=peer, device_id_type=MESH)

    pl.semaphore_wait(barrier, len(AROUND) + len(peers))
    take_r = {-1: pl.ds(0, 3), 0: pl.ds(0, ROWS), 1: pl.ds(ROWS - 3, 3)}
    take_c = {-1: pl.ds(0, 16), 0: pl.ds(0, COLS), 1: pl.ds(COLS - 16, 16)}
    land_r = {-1: pl.ds(ROWS + 3, 3), 0: pl.ds(3, ROWS), 1: pl.ds(0, 3)}
    land_c = {-1: pl.ds(COLS + 16, 16), 0: pl.ds(16, COLS), 1: pl.ds(0, 16)}
    halo = []
    for i, (dl, dg) in enumerate(AROUND):
        copy = pltpu.make_async_remote_copy(
            src_ref=feat.at[take_r[dg], take_c[dl]],
            dst_ref=f_ref.at[land_r[dg], land_c[dl]],
            send_sem=halo_send.at[i],
            recv_sem=halo_recv.at[i],
            device_id=near(dl, dg),
            device_id_type=MESH,
        )
        copy.start()
        halo.append(copy)
    f_ref[3 : 3 + ROWS, 16 : 16 + COLS, :] = feat[...]

    for a in range(3):
        for b in range(3):
            rows, cols = slice(a * CH, (a + 1) * CH), slice(b * CH, (b + 1) * CH)
            w1c[rows, cols] = w1[a, b]
            w2c[rows, cols] = w2[a, b]
            w2f[cols, rows] = w2[2 - a, 2 - b]
    v1f[...] = jnp.zeros_like(v1f)
    wof[...] = jnp.zeros_like(wof)
    for a in range(3):
        for b in range(3):
            for c in range(3):
                v1f[a * 32 + b * 8 + c : a * 32 + b * 8 + c + 1, :] = v1w[c, a, b : b + 1].astype(F32)
            wof[a, b * 8 : b * 8 + 3, :] = wo[a, b].astype(F32)
            v2c[:, (a * 3 + b) * VW : (a * 3 + b + 1) * VW] = v2w[a, b]
            v2t[:, (a * 3 + b) * VW : (a * 3 + b + 1) * VW] = (
                v2w[2 - a, 2 - b].astype(F32).T.astype(BF)
            )
    v1 = v1f[...].T.astype(BF)
    v1b_col = v1b[...].reshape(VW, 1)
    v2b_col = v2b[...].reshape(VW, 1)
    lin_col = lin[...].reshape(VW, 1)

    zs[:, 0:128] = jnp.zeros((32, 128), BF)
    zs[:, PIX + 128 :] = jnp.zeros((32, 128), BF)
    for ref in (fs, gs):
        ref[:, :, 0:128] = jnp.zeros((3, VW, 128), BF)
        ref[:, :, PIX + 128 :] = jnp.zeros((3, VW, 128), BF)
    y_ref[:, 0:128] = jnp.zeros((72, 128), F32)
    y_ref[:, PIX + 128 :] = jnp.zeros((72, 128), F32)
    pb[:, :, 0:8, :] = jnp.zeros((3, 3, 8, 128), F32)
    pb[:, :, 16:24, :] = jnp.zeros((3, 3, 8, 128), F32)
    own_e[...] = jnp.zeros_like(own_e)
    all_e[...] = jnp.zeros_like(all_e)

    for r in range(TROWS):
        tgt = target[:, r, :].astype(F32)
        unit_t[0:8, r * 128 : (r + 1) * 128] = jnp.concatenate(
            [tgt, jnp.zeros((5, 128), F32)], axis=0
        )

    @pl.loop(0, 8, unroll=4)
    def _(k):
        store_scaled(zs, unit_t[0:8, span(k * 1024, 1024, 128)], k * 8, 8)

    vgg_first(zs, fs, v1, v1b_col, 4)

    @pl.loop(0, 8, unroll=4)
    def _(k):
        at = span(k * 1024, 1024, 128)
        index = tap_i[:, at]
        weight = tap_w[:, at]
        column = lax.shift_left(lax.shift_right_logical(index, 10), 7) + jnp.bitwise_and(index, 127)
        slot = jnp.bitwise_and(lax.shift_right_logical(index, 7), 7)
        left = jnp.min(column, axis=0, keepdims=True)
        top = jnp.min(slot, axis=0, keepdims=True)
        is_left, is_top = column == left, slot == top

        def corner(cond):
            return jnp.sum(jnp.where(cond, weight, 0.0), axis=0, keepdims=True)

        not_left, not_top = jnp.logical_not(is_left), jnp.logical_not(is_top)
        w_tl, w_tr = corner(is_top & is_left), corner(is_top & not_left)
        w_bl, w_br = corner(not_top & is_left), corner(not_top & not_left)
        j = lax.broadcasted_iota(jnp.int32, (8, 1024), 0)
        on_top, on_next = j == top, j == top + 1
        al[:, at] = jnp.where(on_top, w_tl, jnp.where(on_next, w_bl, 0.0))
        ar[:, at] = jnp.where(on_top, w_tr, jnp.where(on_next, w_br, 0.0))
        x = lax.broadcasted_iota(jnp.int32, (384, 1024), 0)
        hot[:, at] = jnp.where(x == left, 1.0, 0.0).astype(BF)

    for copy in halo:
        copy.wait()
    north, south = grp == 0, grp == n_grp - 1

    @pl.loop(0, ROWS + 6, unroll=2)
    def _(r):
        a0[r] = act_slope(f_ref[r])[0]

    def clear(ref, rows):
        @pl.when(north)
        def _():
            ref[0:rows] = jnp.zeros((rows, WIDE, CH), BF)

        @pl.when(south)
        def _():
            ref[ref.shape[0] - rows :] = jnp.zeros((rows, WIDE, CH), BF)

    clear(a0, 3)

    @pl.loop(0, 5, unroll=5)
    def _(k):
        r = k * 4
        h = (conv_rows(a0, w1c[...], r, 4) + b1[...]).astype(BF)
        act, slope = act_slope(h)
        a1[pl.ds(r, 4)] = act.reshape(4, WIDE, CH)
        s1[pl.ds(r, 4)] = slope.reshape(4, WIDE, CH)

    clear(a1, 2)

    @pl.loop(0, 6, unroll=3)
    def _(k):
        r = k * 3
        f = f_ref[pl.ds(r + 2, 3)].reshape(3 * WIDE, CH).astype(F32)
        h = (f + conv_rows(a1, w2c[...], r, 3) + b2[...]).astype(BF)
        act, slope = act_slope(h)
        a2[pl.ds(r, 3)] = act.reshape(3, WIDE, CH)
        s2[pl.ds(r, 3)] = slope.reshape(3, WIDE, CH)

    clear(a2, 1)

    wo_cat = jnp.concatenate([wof[a] for a in range(3)], axis=1).astype(BF)
    for r in range(ROWS):
        rhs = jnp.concatenate([a2[r + a] for a in range(3)], axis=1)
        z = dot(wo_cat, rhs, 1, 1)
        colour = z[0:8, 15 : 15 + COLS] + z[8:16, 16 : 16 + COLS] + z[16:24, 17 : 17 + COLS]
        for c in range(3):
            c_own[c, r : r + 1, :] = colour[c : c + 1] + bo[c]

    colours = []
    for i, dl in enumerate((-1, 1)):
        copy = pltpu.make_async_remote_copy(
            src_ref=c_own,
            dst_ref=c_near.at[1 - i],
            send_sem=col_send.at[i],
            recv_sem=col_recv.at[1 - i],
            device_id=near(dl, 0),
            device_id_type=MESH,
        )
        copy.start()
        colours.append(copy)

    @pl.loop(0, TROWS // 4, unroll=4)
    def _(k):
        f = jnp.maximum(dot(v2c[...], nine_taps(fs, k * 4, 4)) + v2b_col, 0.0)
        unit_t[:, span(k * 512, 512, 128)] = f * inv_norm(f)

    for copy in colours:
        copy.wait()

    start = rows_ref[1, 0, 0]
    slabs = (c_near.at[0], c_own, c_near.at[1])
    table = jnp.concatenate(
        [
            jnp.concatenate([slab[c, pl.ds(start, 8), :] for c in range(3)], axis=0)
            for slab in slabs
        ],
        axis=1,
    )
    table = jnp.concatenate([table, pltpu.roll(table, 383, 1)], axis=0)
    table_hi = table.astype(BF)
    table_lo = (table - table_hi.astype(F32)).astype(BF)
    table = jnp.concatenate([table_hi, table_lo], axis=0)

    @pl.loop(0, 8, unroll=4)
    def _(k):
        at = span(k * 1024, 1024, 128)
        got = dot(table, hot[:, at])
        got = got[0:48] + got[48:96]
        w_left, w_right = al[:, at], ar[:, at]
        picture = [
            jnp.sum(
                got[c * 8 : c * 8 + 8] * w_left + got[24 + c * 8 : 32 + c * 8] * w_right,
                axis=0,
                keepdims=True,
            )
            for c in range(3)
        ]
        picture = jnp.concatenate(picture + [jnp.zeros((5, 1024), F32)], axis=0)
        store_scaled(zs, picture, k * 8, 8)

    vgg_first(zs, fs, v1, v1b_col, 4)
    loss_acc[...] = jnp.zeros_like(loss_acc)

    @pl.loop(0, TROWS // 4, unroll=4)
    def _(k):
        f = jnp.maximum(dot(v2c[...], nine_taps(fs, k * 4, 4)) + v2b_col, 0.0)
        inv = inv_norm(f)
        u = f * inv
        diff = u - unit_t[:, span(k * 512, 512, 128)]
        weighted = lin_col * diff
        loss_acc[...] += jnp.sum(weighted * diff, axis=0, keepdims=True)
        g = weighted * (2.0 * LOSS_SCALE / PIX)
        g = inv * (g - u * jnp.sum(g * u, axis=0, keepdims=True))
        shift_store(gs, jnp.where(f > 0.0, g, 0.0), k * 4, 4)

    loss = jnp.sum(loss_acc[...], axis=1, keepdims=True) * (1.0 / PIX)
    grads[REST + 96 : REST + 104, :] = jnp.broadcast_to(loss, (8, 128))
    grads[18 * CH + 104 :, :] = jnp.zeros((GRAD_ROWS - 18 * CH - 104, CH), F32)
    for p in range(3):
        line_sum[p, SHARE:] = jnp.zeros((128 - SHARE, CH), F32)

    v1_back = jnp.concatenate(
        [
            v1f[(2 - a) * 32 + (2 - b) * 8 : (2 - a) * 32 + (2 - b) * 8 + 8, :]
            for b in range(3)
            for a in range(3)
        ],
        axis=0,
    ).astype(BF)

    @pl.loop(0, TROWS // 4, unroll=4)
    def _(k):
        g = dot(v2t[...], nine_taps(gs, k * 4, 4)).astype(BF)
        at = span((k * 4 + 1) * 128, 512, 128)
        g = jnp.where(fs[1, :, at] > 0, g, jnp.zeros_like(g))
        y_ref[:, at] = dot(v1_back, g)

    def table_adjoint(k, acc):
        at = span(k * 1024, 1024, 128)
        part = []
        for b in range(3):
            part.append(
                sum(
                    y_ref[(b * 3 + a) * 8 : (b * 3 + a) * 8 + 8, span((k * 8 + a) * 128, 1024, 128)]
                    for a in range(3)
                )
            )
        col = jnp.bitwise_and(lax.broadcasted_iota(jnp.int32, (8, 1024), 1), 127)
        dz = (
            jnp.where(col > 0, pltpu.roll(part[0], 1, 1), 0.0)
            + part[1]
            + jnp.where(col < 127, pltpu.roll(part[2], 1023, 1), 0.0)
        )
        dz = dz.astype(BF).astype(F32) / per_channel(SPREAD)
        spread = jnp.concatenate(
            [w[:, at] * dz[c : c + 1] for w in (al, ar) for c in range(3)], axis=0
        )
        hi = spread.astype(BF)
        lo = (spread - hi.astype(F32)).astype(BF)
        return acc + dot(jnp.concatenate([hi, lo], axis=0), hot[:, at], 1, 1)

    acc = lax.fori_loop(0, 8, table_adjoint, jnp.zeros((96, 384), F32), unroll=4)
    acc = acc[0:48] + acc[48:96]
    adjoint = acc[0:24] + pltpu.roll(acc[24:48], 1, 1)
    for k in range(3):
        for c in range(3):
            tb[k, c] = adjoint[c * 8 : c * 8 + 8, k * 128 : (k + 1) * 128]
    pb[1, :, 8:16, :] = tb[1]

    returned = []
    for i, (k, dl) in enumerate(((0, -1), (2, 1))):
        copy = pltpu.make_async_remote_copy(
            src_ref=tb.at[k],
            dst_ref=pb.at[k, :, pl.ds(8, 8), :],
            send_sem=tab_send.at[i],
            recv_sem=tab_recv.at[i],
            device_id=near(dl, 0),
            device_id_type=MESH,
        )
        copy.start()
        returned.append(copy)
    def turn(act, turned, first_row):
        @pl.loop(0, ROWS + 2, unroll=3)
        def _(r):
            block = act[r + first_row].astype(F32).T
            at = span(r * 128, 128, 128)
            for b in range(3):
                turned[b, :, at] = block[:, 15 + b : 15 + b + COLS].astype(BF)

    turn(a1, t1, 1)
    for copy in returned:
        copy.wait()

    for c in range(3):
        placed = sum(pb[k, c, pl.ds(8 - rows_ref[k, 0, 0], ROWS), :] for k in range(3))
        ca[c] = placed.astype(BF)

    exchanged = []
    for i, (dl, dg) in enumerate(AROUND):
        copy = pltpu.make_async_remote_copy(
            src_ref=ca,
            dst_ref=ca_near.at[7 - i],
            send_sem=adj_send.at[i],
            recv_sem=adj_recv.at[7 - i],
            device_id=near(dl, dg),
            device_id_type=MESH,
        )
        copy.start()
        exchanged.append(copy)

    def taps_of(target_e, c, field):
        for b in range(3):
            moved = pltpu.roll(field, 384 - (111 + 2 - b), 1)[:, 0:256]
            target_e[:, b * 8 + c, :] = moved

    def patches(source_e, r):
        return jnp.concatenate([source_e[r + a] for a in range(3)], axis=0)[:, :WIDE].astype(BF)

    rows2 = jnp.zeros((2, 384), F32)
    own = [ca[c].astype(F32) for c in range(3)]
    for c in range(3):
        side = jnp.zeros((ROWS, 128), F32)
        middle = jnp.concatenate([side, own[c], side], axis=1)
        taps_of(own_e, c, jnp.concatenate([rows2, middle, rows2], axis=0))
    grad_out = jnp.zeros((96, CH), F32)
    for r in range(ROWS + 2):
        grad_out += dot(patches(own_e, r), a2[r])
    for a in range(3):
        base = REST + (2 - a) * 32
        grads[base : base + 32, :] = grad_out[a * 32 : a * 32 + 32]

    turn(a0, t0, 2)
    for copy in exchanged:
        copy.wait()
    at_of = {delta: i for i, delta in enumerate(AROUND)}
    has_north = jnp.where(north, 0.0, 1.0)
    has_south = jnp.where(south, 0.0, 1.0)
    for c in range(3):

        def line(dg):
            parts = [
                own[c] if (dl, dg) == (0, 0) else ca_near[at_of[(dl, dg)], c].astype(F32)
                for dl in (-1, 0, 1)
            ]
            return jnp.concatenate(parts, axis=1)

        field = jnp.concatenate(
            [line(-1)[ROWS - 2 :] * has_north, line(0), line(1)[0:2] * has_south], axis=0
        )
        taps_of(all_e, c, field)

    wo_flip = jnp.concatenate([wof[2 - a] for a in range(3)], axis=0).astype(BF)
    for r in range(ROWS + 2):
        d2[r] = (dot(patches(all_e, r), wo_flip, 0, 0) * s2[r]).astype(BF)
    clear(d2, 1)

    def weight_grad(turned, adj, base, taps):
        for tap in taps:
            a, b = tap // 3, tap % 3
            at = base + tap * CH
            grads[at : at + CH, :] = dot(turned[b, :, a * 128 : a * 128 + ROWS * 128], adj)

    weight_grad(t1, d2[1 : 1 + ROWS, 16 : 16 + COLS, :].reshape(ROWS * COLS, CH), 0, range(9))
    first = scatter_part(0, grads, line_in, sum_sems)

    @pl.loop(0, 4, unroll=4)
    def _(k):
        r = k * 4
        g = conv_rows(d2, w2f[...], r, 4, 1) * s1[pl.ds(r + 2, 4)].reshape(4 * WIDE, CH)
        d1[pl.ds(r, 4)] = g.reshape(4, WIDE, CH)[:, 16 : 16 + COLS].astype(BF)

    d1_all = d1[...].reshape(ROWS * COLS, CH)
    weight_grad(t0, d1_all, ONE, range(0, 4))
    first += scatter_part(1, grads, line_in, sum_sems)
    weight_grad(t0, d1_all, ONE, range(4, 9))
    first += scatter_part(2, grads, line_in, sum_sems)

    sum_all(first, grads, total, line_in, line_sum, plane_in, plane_sum, gathered, sum_sems)
    outs = []
    for i, (out, at, size) in enumerate(
        ((one_out, ONE, 9 * CH), (two_out, 0, 9 * CH), (rest_out, REST, 104))
    ):
        copy = pltpu.make_async_copy(total.at[at : at + size], out, out_sem.at[i])
        copy.start()
        outs.append(copy)
    for copy in outs:
        copy.wait()


def run_kernel(*args):
    vmem = pl.BlockSpec(memory_space=pltpu.VMEM)
    smem = pl.BlockSpec(memory_space=pltpu.SMEM)
    specs = [vmem] * 16
    specs[6] = smem
    specs[12] = smem
    dma = pltpu.SemaphoreType.DMA
    return pl.pallas_call(
        kernel,
        out_shape=(
            jax.ShapeDtypeStruct((9 * CH, CH), F32),
            jax.ShapeDtypeStruct((9 * CH, CH), F32),
            jax.ShapeDtypeStruct((104, CH), F32),
        ),
        in_specs=specs,
        out_specs=(pl.BlockSpec(memory_space=pl.ANY),) * 3,
        scratch_shapes=[
            pltpu.VMEM((ROWS + 6, WIDE, CH), BF),
            pltpu.VMEM((ROWS + 6, WIDE, CH), BF),
            pltpu.VMEM((ROWS + 4, WIDE, CH), BF),
            pltpu.VMEM((ROWS + 2, WIDE, CH), BF),
            pltpu.VMEM((ROWS + 4, WIDE, CH), F32),
            pltpu.VMEM((ROWS + 2, WIDE, CH), F32),
            pltpu.VMEM((3 * CH, 3 * CH), BF),
            pltpu.VMEM((3 * CH, 3 * CH), BF),
            pltpu.VMEM((3 * CH, 3 * CH), BF),
            pltpu.VMEM((3, ROWS, COLS), F32),
            pltpu.VMEM((2, 3, ROWS, COLS), F32),
            pltpu.VMEM((384, PIX), BF),
            pltpu.VMEM((8, PIX), F32),
            pltpu.VMEM((8, PIX), F32),
            pltpu.VMEM((96, VW), F32),
            pltpu.VMEM((VW, 9 * VW), BF),
            pltpu.VMEM((VW, 9 * VW), BF),
            pltpu.VMEM((32, PIX + 256), BF),
            pltpu.VMEM((3, VW, PIX + 256), BF),
            pltpu.VMEM((3, VW, PIX + 256), BF),
            pltpu.VMEM((VW, PIX), F32),
            pltpu.VMEM((72, PIX + 256), F32),
            pltpu.VMEM((3, 3, 8, 128), F32),
            pltpu.VMEM((3, 3, 24, 128), F32),
            pltpu.VMEM((3, ROWS, COLS), BF),
            pltpu.VMEM((8, 3, ROWS, COLS), BF),
            pltpu.VMEM((ROWS + 4, 32, 256), F32),
            pltpu.VMEM((ROWS + 4, 32, 256), F32),
            pltpu.VMEM((ROWS + 2, WIDE, CH), BF),
            pltpu.VMEM((ROWS, COLS, CH), BF),
            pltpu.VMEM((3, CH, (ROWS + 2) * COLS), BF),
            pltpu.VMEM((3, CH, (ROWS + 2) * COLS), BF),
            pltpu.VMEM((1, 512), F32),
            pltpu.VMEM((3, 32, CH), F32),
            pltpu.VMEM((GRAD_ROWS, CH), F32),
            pltpu.VMEM((GRAD_ROWS, CH), F32),
            pltpu.VMEM((3, 7, SHARE, CH), F32),
            pltpu.VMEM((3, 128, CH), F32),
            pltpu.VMEM((3, 15, 8, CH), F32),
            pltpu.VMEM((3, 8, CH), F32),
            pltpu.VMEM((3, 128, CH), F32),
            dma((8,)), dma((8,)), dma((2,)), dma((2,)), dma((2,)), dma((2,)), dma((8,)), dma((8,)), dma((3,)),
            dma((3, 7)), dma((3, 7)), dma((3, 15)), dma((3, 15)),
            dma((3, 15)), dma((3, 15)), dma((3, 7)), dma((3, 7)),
        ],
        compiler_params=pltpu.CompilerParams(
            collective_id=0, has_side_effects=True, vmem_limit_bytes=56 * 1024 * 1024
        ),
    )(*args)


def hand_over_kernel(one, two, rest, loss, one_out, two_out, grad_out, sems):
    copies = []
    for i, (src, dst) in enumerate(((one, one_out), (two, two_out))):
        copy = pltpu.make_async_copy(src, dst, sems.at[i])
        copy.start()
        copies.append(copy)
    for a in range(3):
        for b in range(3):
            grad_out[a, b] = rest[a * 32 + b * 8 : a * 32 + b * 8 + 3, :]
    loss[...] = rest[96:97, 0:1]
    for copy in copies:
        copy.wait()


def hand_over(one, two, rest):
    vmem, hbm = pl.BlockSpec(memory_space=pltpu.VMEM), pl.BlockSpec(memory_space=pl.ANY)
    block = jax.ShapeDtypeStruct((9 * CH, CH), F32)
    return pl.pallas_call(
        hand_over_kernel,
        out_shape=(
            jax.ShapeDtypeStruct((1, 1), F32),
            block,
            block,
            jax.ShapeDtypeStruct((3, 3, 3, CH), F32),
        ),
        in_specs=[vmem, vmem, vmem],
        out_specs=(vmem, hbm, hbm, vmem),
        scratch_shapes=[pltpu.SemaphoreType.DMA((2,))],
    )(one, two, rest)


def per_device(
    features,
    conv_one_w,
    conv_one_b,
    conv_two_w,
    conv_two_b,
    out_conv_w,
    out_conv_b,
    vgg_one_w,
    vgg_one_b,
    vgg_two_w,
    vgg_two_b,
    lin_weights,
    row_lists,
    tap_index,
    tap_weight,
    target_tiles,
):
    grad_one, grad_two, rest = run_kernel(
        features,
        conv_one_w,
        conv_one_b.reshape(1, CH),
        conv_two_w,
        conv_two_b.reshape(1, CH),
        jnp.transpose(out_conv_w, (0, 1, 3, 2)),
        out_conv_b,
        jnp.transpose(vgg_one_w, (1, 2, 3, 0)),
        vgg_one_b.reshape(1, VW),
        jnp.transpose(vgg_two_w, (2, 3, 0, 1)),
        vgg_two_b.reshape(1, VW),
        lin_weights.reshape(1, VW),
        jnp.transpose(row_lists, (1, 0, 2)),
        tap_index[0],
        tap_weight[0],
        target_tiles[0],
    )
    loss, grad_one, grad_two, grad_out = hand_over(grad_one, grad_two, rest)
    return (
        loss.reshape(()),
        grad_one.reshape(3, 3, CH, CH),
        grad_two.reshape(3, 3, CH, CH),
        jnp.transpose(grad_out, (0, 1, 3, 2)),
    )


def solution(mesh):
    in_specs = (
        P("grp", "lon", None),
        P(),
        P(),
        P(),
        P(),
        P(),
        P(),
        P(),
        P(),
        P(),
        P(),
        P(),
        P(("lon", "grp"), None, None),
        P(("lon", "grp"), None, None),
        P(("lon", "grp"), None, None),
        P(("lon", "grp"), None, None, None),
    )
    out_specs = (P(), P(), P(), P())
    return jax.shard_map(
        per_device, mesh=mesh, in_specs=in_specs, out_specs=out_specs, check_vma=False
    )
```

```python
import jax
import jax.numpy as jnp
from jax import lax
from jax.experimental import pallas as pl
from jax.experimental.pallas import tpu as pltpu
from jax.sharding import PartitionSpec as P

OFFSET = (-0.03, -0.088, -0.188)
SPREAD = (0.458, 0.448, 0.45)
LOSS_SCALE = 64.0

CH = 128
VW = 64
ROWS = 16
COLS = 128
WIDE = 160
TROWS = 64
PIX = TROWS * 128
BF = jnp.bfloat16
F32 = jnp.float32
MESH = pl.DeviceIdType.MESH

AROUND = ((-1, -1), (-1, 0), (-1, 1), (0, -1), (0, 1), (1, -1), (1, 0), (1, 1))


PARTS = ((0, (1, 2)), (1, (0, 2)), (2, (0, 1)))
GRAD_ROWS = 2496
REST = 9 * CH
ONE = 9 * CH + 104
PART = GRAD_ROWS // 3
SHARE = PART // 8
LINE_STEPS = [(d, k) for d in range(4) for k in range(2) if (d, k) != (0, 0)]
PLANE_STEPS = [(d, e) for d in range(4) for e in range(4) if (d, e) != (0, 0)]


def place():
    lon, grp = lax.axis_index("lon"), lax.axis_index("grp")
    return (lon // 8, (lon % 2) * 2 + grp // 2, (lon // 2) % 4), grp % 2


def device(xyz, core):
    x, y, z = xyz
    return ((x * 4 + z) * 2 + y // 2, (y % 2) * 2 + core)


def line_peers(axis):
    xyz, core = place()
    for d, k in LINE_STEPS:
        at, its_core = (xyz[axis] + d) % 4, (core + k) % 2
        peer = tuple(at if i == axis else xyz[i] for i in range(3))
        yield device(peer, its_core), at * 2 + its_core


def plane_peers(axes):
    xyz, core = place()
    u, v = axes
    for d, e in PLANE_STEPS:
        at_u, at_v = (xyz[u] + d) % 4, (xyz[v] + e) % 4
        peer = tuple(at_u if i == u else at_v if i == v else xyz[i] for i in range(3))
        yield device(peer, core), at_u * 4 + at_v


def sum_offsets():
    found = set()
    for axis, axes in PARTS:
        for d, k in LINE_STEPS:
            found.add(tuple(d if i == axis else 0 for i in range(3)) + (k,))
        for d, e in PLANE_STEPS:
            found.add(tuple(d if i == axes[0] else e if i == axes[1] else 0 for i in range(3)) + (0,))
    return sorted(found)


def rows8(start, size):
    return pl.ds(pl.multiple_of(start, 8), size)


def send(src, dst, send_sem, recv_sem, to):
    copy = pltpu.make_async_remote_copy(
        src_ref=src, dst_ref=dst, send_sem=send_sem, recv_sem=recv_sem, device_id=to, device_id_type=MESH
    )
    copy.start()
    return copy


def scatter_part(p, grads, line_in, sems):
    copies = []
    for i, (peer, index) in enumerate(line_peers(PARTS[p][0])):
        src = grads.at[rows8(p * PART + index * SHARE, SHARE)]
        copies.append(send(src, line_in.at[p, i], sems[0].at[p], sems[1].at[p], peer))
    return copies


def sum_all(first, grads, out, line_in, line_sum, plane_in, plane_sum, gathered, sems):
    ls, lr, ps, pr, gs, gr, os, orr = sems

    def all_of(ref, sem):
        pltpu.make_async_copy(ref, ref, sem).wait()

    xyz, core = place()
    second = []
    for p, (axis, axes) in enumerate(PARTS):
        mine = xyz[axis] * 2 + core
        all_of(line_in.at[p], lr.at[p])
        total = grads[rows8(p * PART + mine * SHARE, SHARE), :]
        for i in range(7):
            total = total + line_in[p, i]
        line_sum[p, 0:SHARE] = total
        for i, (peer, index) in enumerate(plane_peers(axes)):
            src = line_sum.at[p, rows8(index * 8, 8)]
            second.append(send(src, plane_in.at[p, i], ps.at[p], pr.at[p], peer))
    third = []
    for p, (axis, axes) in enumerate(PARTS):
        mine = xyz[axes[0]] * 4 + xyz[axes[1]]
        all_of(plane_in.at[p], pr.at[p])
        total = line_sum[p, rows8(mine * 8, 8), :]
        for i in range(15):
            total = total + plane_in[p, i]
        plane_sum[p] = total
        gathered[p, rows8(mine * 8, 8), :] = total
        for i, (peer, index) in enumerate(plane_peers(axes)):
            dst = gathered.at[p, rows8(mine * 8, 8)]
            third.append(send(plane_sum.at[p], dst, gs.at[p], gr.at[p], peer))
    fourth = []
    for p, (axis, axes) in enumerate(PARTS):
        mine = xyz[axis] * 2 + core
        at = rows8(p * PART + mine * SHARE, SHARE)
        all_of(gathered.at[p, 0:120], gr.at[p])
        for i, (peer, index) in enumerate(line_peers(axis)):
            fourth.append(send(gathered.at[p, 0:SHARE], out.at[at], os.at[p], orr.at[p], peer))
        out[at, :] = gathered[p, 0:SHARE]
    for p in range(3):
        all_of(line_in.at[p], ls.at[p])
        all_of(plane_in.at[p], ps.at[p])
        all_of(gathered.at[p, 0:120], gs.at[p])
    for p in range(3):
        all_of(out.at[0 : 7 * SHARE], os.at[p])
        all_of(out.at[0 : 7 * SHARE], orr.at[p])


HALO_ORDER = (1, 6, 3, 4, 0, 2, 5, 7)


def dot(a, b, ca=1, cb=0):
    return lax.dot_general(a, b, (((ca,), (cb,)), ((), ())), preferred_element_type=F32)


def span(start, size, unit):
    if isinstance(start, int):
        return pl.ds(start, size)
    return pl.ds(pl.multiple_of(start, unit), size)


def ext(delta, low, high):
    return low if delta < 0 else high


def conv_rows(src, weight, r, n, last=0):
    lhs = jnp.concatenate(
        [src[pl.ds(r + a, n)].reshape(n * WIDE, CH) for a in range(3)], axis=1
    )
    z = dot(lhs, weight, 1, last)
    return (
        pltpu.roll(z[:, :CH], 1, 0)
        + z[:, CH : 2 * CH]
        + pltpu.roll(z[:, 2 * CH :], n * WIDE - 1, 0)
    )


def act_slope(hidden):
    h = hidden.astype(F32)
    s = jax.nn.sigmoid(h)
    return (h * s).astype(BF), s * (1.0 + h * (1.0 - s))


def lane_masks(n):
    col = lax.broadcasted_iota(jnp.int32, (1, 128), 1)
    return col > 0, col < 127


def shift_store(ref, y, row0, n):
    first, last = lane_masks(n)
    for r in range(n):
        part = y[:, r * 128 : (r + 1) * 128]
        at = span((row0 + r + 1) * 128, 128, 128)
        ref[0, :, at] = jnp.where(first, pltpu.roll(part, 1, 1), 0.0).astype(BF)
        ref[1, :, at] = part.astype(BF)
        ref[2, :, at] = jnp.where(last, pltpu.roll(part, 127, 1), 0.0).astype(BF)


def per_channel(values):
    row = lax.broadcasted_iota(jnp.int32, (8, 1), 0)
    out = jnp.full((8, 1), values[2], F32)
    out = jnp.where(row == 0, values[0], out)
    return jnp.where(row == 1, values[1], out)


def store_scaled(zs, colours, row0, n):
    row = lax.broadcasted_iota(jnp.int32, (8, 1), 0)
    z = jnp.where(row < 3, (colours - per_channel(OFFSET)) / per_channel(SPREAD), 0.0)
    first, last = lane_masks(n)
    for r in range(n):
        part = z[:, r * 128 : (r + 1) * 128]
        stack = jnp.concatenate(
            [
                jnp.where(first, pltpu.roll(part, 1, 1), 0.0),
                part,
                jnp.where(last, pltpu.roll(part, 127, 1), 0.0),
                jnp.zeros_like(part),
            ],
            axis=0,
        )
        zs[:, span((row0 + r + 1) * 128, 128, 128)] = stack.astype(BF)


def vgg_first(zs, fs, v1, v1b, n):
    @pl.loop(0, TROWS // n, unroll=4)
    def _(k):
        r0 = k * n
        rhs = jnp.concatenate(
            [zs[:, span((r0 + a) * 128, n * 128, 128)] for a in range(3)], axis=0
        )
        y = jnp.maximum(dot(v1, rhs) + v1b, 0.0)
        shift_store(fs, y, r0, n)


def nine_taps(ref, r0, n):
    return jnp.concatenate(
        [ref[b, :, span((r0 + a) * 128, n * 128, 128)] for a in range(3) for b in range(3)], axis=0
    )


def inv_norm(f):
    return lax.rsqrt(jnp.sum(f * f, axis=0, keepdims=True) + 1e-05)


def kernel(
    feat, w1, b1, w2, b2, wo, bo, v1w, v1b, v2w, v2b, lin, rows_ref, tap_i, tap_w, target,
    one_out, two_out, rest_out,
    f_ref, a0, a1, a2, s1, s2, w1c, w2c, w2f, c_own, c_near, hot, al, ar, v1f, v2c, v2t,
    zs, fs, gs, unit_t, y_ref, tb, pb, ca, ca_near, own_e, all_e, d2, d1, t0, t1, loss_acc, wof,
    side_out, side_in, grads, total, line_in, line_sum, plane_in, plane_sum, gathered,
    halo_send, halo_recv, col_send, col_recv, tab_send, tab_recv, adj_send, adj_recv, out_sem,
    *sum_sems,
):
    lon, grp = lax.axis_index("lon"), lax.axis_index("grp")
    n_lon, n_grp = lax.axis_size("lon"), lax.axis_size("grp")

    def near(dl, dg):
        return (lax.rem(lon + dl + n_lon, n_lon), lax.rem(grp + dg + n_grp, n_grp))

    barrier = pltpu.get_barrier_semaphore()
    for dl, dg in AROUND:
        pl.semaphore_signal(barrier, inc=1, device_id=near(dl, dg), device_id_type=MESH)
    xyz, core = place()
    peers = sum_offsets()
    for off in peers:
        peer = device([(xyz[i] + off[i]) % 4 for i in range(3)], (core + off[3]) % 2)
        pl.semaphore_signal(barrier, inc=1, device_id=peer, device_id_type=MESH)

    @pl.loop(0, 8, unroll=4)
    def _(k):
        at = span(k * 1024, 1024, 128)
        index = tap_i[:, at]
        weight = tap_w[:, at]
        column = lax.shift_left(lax.shift_right_logical(index, 10), 7) + jnp.bitwise_and(index, 127)
        slot = jnp.bitwise_and(lax.shift_right_logical(index, 7), 7)
        left = jnp.min(column, axis=0, keepdims=True)
        top = jnp.min(slot, axis=0, keepdims=True)
        is_left, is_top = column == left, slot == top

        def corner(cond):
            return jnp.sum(jnp.where(cond, weight, 0.0), axis=0, keepdims=True)

        not_left, not_top = jnp.logical_not(is_left), jnp.logical_not(is_top)
        w_tl, w_tr = corner(is_top & is_left), corner(is_top & not_left)
        w_bl, w_br = corner(not_top & is_left), corner(not_top & not_left)
        j = lax.broadcasted_iota(jnp.int32, (8, 1024), 0)
        on_top, on_next = j == top, j == top + 1
        al[:, at] = jnp.where(on_top, w_tl, jnp.where(on_next, w_bl, 0.0))
        ar[:, at] = jnp.where(on_top, w_tr, jnp.where(on_next, w_br, 0.0))
        x = lax.broadcasted_iota(jnp.int32, (384, 1024), 0)
        hot[:, at] = jnp.where(x == left, 1.0, 0.0).astype(BF)

    side_out[0] = feat[:, 0:8, :].astype(F32).reshape(ROWS * 8, CH).astype(BF)
    side_out[1] = feat[:, COLS - 8 :, :].astype(F32).reshape(ROWS * 8, CH).astype(BF)
    pl.semaphore_wait(barrier, len(AROUND) + len(peers))
    take_r = {-1: pl.ds(0, 3), 1: pl.ds(ROWS - 3, 3)}
    take_c = {-1: pl.ds(0, 16), 0: pl.ds(0, COLS), 1: pl.ds(COLS - 16, 16)}
    land_r = {-1: pl.ds(ROWS + 3, 3), 1: pl.ds(0, 3)}
    land_c = {-1: pl.ds(COLS + 16, 16), 0: pl.ds(16, COLS), 1: pl.ds(0, 16)}
    north, south = grp == 0, grp == n_grp - 1
    sends = {-1: grp > 0, 0: None, 1: grp < n_grp - 1}
    lands = {-1: sends[1], 0: None, 1: sends[-1]}

    def only_if(cond, act):
        if cond is None:
            act()
        else:
            pl.when(cond)(act)

    halo = []
    for i in HALO_ORDER:
        dl, dg = AROUND[i]
        if dg == 0:
            src, dst = side_out.at[(1 + dl) // 2], side_in.at[(1 + dl) // 2]
        else:
            src = feat.at[take_r[dg], take_c[dl]]
            dst = f_ref.at[land_r[dg], land_c[dl]]
        copy = pltpu.make_async_remote_copy(
            src_ref=src,
            dst_ref=dst,
            send_sem=halo_send.at[i],
            recv_sem=halo_recv.at[i],
            device_id=near(dl, dg),
            device_id_type=MESH,
        )
        only_if(sends[dg], copy.start)
        halo.append((dg, copy))
    f_ref[3 : 3 + ROWS, 16 : 16 + COLS, :] = feat[...]

    for a in range(3):
        for b in range(3):
            rows, cols = slice(a * CH, (a + 1) * CH), slice(b * CH, (b + 1) * CH)
            w1c[rows, cols] = w1[a, b]
            w2c[rows, cols] = w2[a, b]
            w2f[cols, rows] = w2[2 - a, 2 - b]
    v1f[...] = jnp.zeros_like(v1f)
    wof[...] = jnp.zeros_like(wof)
    for a in range(3):
        for b in range(3):
            for c in range(3):
                v1f[a * 32 + b * 8 + c : a * 32 + b * 8 + c + 1, :] = v1w[c, a, b : b + 1].astype(F32)
            wof[a, b * 8 : b * 8 + 3, :] = wo[a, b].astype(F32)
            v2c[:, (a * 3 + b) * VW : (a * 3 + b + 1) * VW] = v2w[a, b]
            v2t[:, (a * 3 + b) * VW : (a * 3 + b + 1) * VW] = (
                v2w[2 - a, 2 - b].astype(F32).T.astype(BF)
            )
    v1 = v1f[...].T.astype(BF)
    v1b_col = v1b[...].reshape(VW, 1)
    v2b_col = v2b[...].reshape(VW, 1)
    lin_col = lin[...].reshape(VW, 1)

    zs[:, 0:128] = jnp.zeros((32, 128), BF)
    zs[:, PIX + 128 :] = jnp.zeros((32, 128), BF)
    for ref in (fs, gs):
        ref[:, :, 0:128] = jnp.zeros((3, VW, 128), BF)
        ref[:, :, PIX + 128 :] = jnp.zeros((3, VW, 128), BF)
    y_ref[:, 0:128] = jnp.zeros((72, 128), F32)
    y_ref[:, PIX + 128 :] = jnp.zeros((72, 128), F32)
    pb[:, :, 0:8, :] = jnp.zeros((3, 3, 8, 128), F32)
    pb[:, :, 16:24, :] = jnp.zeros((3, 3, 8, 128), F32)
    own_e[...] = jnp.zeros_like(own_e)
    all_e[...] = jnp.zeros_like(all_e)

    for r in range(TROWS):
        tgt = target[:, r, :].astype(F32)
        unit_t[0:8, r * 128 : (r + 1) * 128] = jnp.concatenate(
            [tgt, jnp.zeros((5, 128), F32)], axis=0
        )

    @pl.loop(0, 8, unroll=4)
    def _(k):
        store_scaled(zs, unit_t[0:8, span(k * 1024, 1024, 128)], k * 8, 8)

    vgg_first(zs, fs, v1, v1b_col, 4)

    a0[3 : 3 + ROWS, 16 : 16 + COLS, :] = act_slope(feat[...])[0]
    for dg, copy in halo:
        only_if(sends[dg], copy.wait_send)
        only_if(lands[dg], copy.wait_recv)
    blank = jnp.zeros((ROWS, 8, CH), F32)
    west = side_in[1].astype(F32).reshape(ROWS, 8, CH)
    east = side_in[0].astype(F32).reshape(ROWS, 8, CH)
    f_ref[3 : 3 + ROWS, 0:16, :] = jnp.concatenate([blank, west], axis=1).astype(BF)
    f_ref[3 : 3 + ROWS, 16 + COLS :, :] = jnp.concatenate([east, blank], axis=1).astype(BF)
    for rows, cols in (
        (slice(0, 3), slice(0, WIDE)),
        (slice(ROWS + 3, ROWS + 6), slice(0, WIDE)),
        (slice(3, ROWS + 3), slice(0, 16)),
        (slice(3, ROWS + 3), slice(16 + COLS, WIDE)),
    ):
        a0[rows, cols, :] = act_slope(f_ref[rows, cols, :])[0]

    def clear(ref, rows):
        @pl.when(north)
        def _():
            ref[0:rows] = jnp.zeros((rows, WIDE, CH), BF)

        @pl.when(south)
        def _():
            ref[ref.shape[0] - rows :] = jnp.zeros((rows, WIDE, CH), BF)

    clear(a0, 3)

    @pl.loop(0, 5, unroll=5)
    def _(k):
        r = k * 4
        h = (conv_rows(a0, w1c[...], r, 4) + b1[...]).astype(BF)
        act, slope = act_slope(h)
        a1[pl.ds(r, 4)] = act.reshape(4, WIDE, CH)
        s1[pl.ds(r, 4)] = slope.reshape(4, WIDE, CH)

    clear(a1, 2)

    @pl.loop(0, 6, unroll=3)
    def _(k):
        r = k * 3
        f = f_ref[pl.ds(r + 2, 3)].reshape(3 * WIDE, CH).astype(F32)
        h = (f + conv_rows(a1, w2c[...], r, 3) + b2[...]).astype(BF)
        act, slope = act_slope(h)
        a2[pl.ds(r, 3)] = act.reshape(3, WIDE, CH)
        s2[pl.ds(r, 3)] = slope.reshape(3, WIDE, CH)

    clear(a2, 1)

    wo_cat = jnp.concatenate([wof[a] for a in range(3)], axis=1).astype(BF)
    for r in range(ROWS):
        rhs = jnp.concatenate([a2[r + a] for a in range(3)], axis=1)
        z = dot(wo_cat, rhs, 1, 1)
        colour = z[0:8, 15 : 15 + COLS] + z[8:16, 16 : 16 + COLS] + z[16:24, 17 : 17 + COLS]
        for c in range(3):
            c_own[c, r : r + 1, :] = colour[c : c + 1] + bo[c]

    colours = []
    for i, dl in enumerate((-1, 1)):
        copy = pltpu.make_async_remote_copy(
            src_ref=c_own,
            dst_ref=c_near.at[1 - i],
            send_sem=col_send.at[i],
            recv_sem=col_recv.at[1 - i],
            device_id=near(dl, 0),
            device_id_type=MESH,
        )
        copy.start()
        colours.append(copy)

    @pl.loop(0, TROWS // 4, unroll=4)
    def _(k):
        f = jnp.maximum(dot(v2c[...], nine_taps(fs, k * 4, 4)) + v2b_col, 0.0)
        unit_t[:, span(k * 512, 512, 128)] = f * inv_norm(f)

    for copy in colours:
        copy.wait()

    start = rows_ref[1, 0, 0]
    slabs = (c_near.at[0], c_own, c_near.at[1])
    table = jnp.concatenate(
        [
            jnp.concatenate([slab[c, pl.ds(start, 8), :] for c in range(3)], axis=0)
            for slab in slabs
        ],
        axis=1,
    )
    table = jnp.concatenate([table, pltpu.roll(table, 383, 1)], axis=0)
    table_hi = table.astype(BF)
    table_lo = (table - table_hi.astype(F32)).astype(BF)
    table = jnp.concatenate([table_hi, table_lo], axis=0)

    @pl.loop(0, 8, unroll=4)
    def _(k):
        at = span(k * 1024, 1024, 128)
        got = dot(table, hot[:, at])
        got = got[0:48] + got[48:96]
        w_left, w_right = al[:, at], ar[:, at]
        picture = [
            jnp.sum(
                got[c * 8 : c * 8 + 8] * w_left + got[24 + c * 8 : 32 + c * 8] * w_right,
                axis=0,
                keepdims=True,
            )
            for c in range(3)
        ]
        picture = jnp.concatenate(picture + [jnp.zeros((5, 1024), F32)], axis=0)
        store_scaled(zs, picture, k * 8, 8)

    vgg_first(zs, fs, v1, v1b_col, 4)
    loss_acc[...] = jnp.zeros_like(loss_acc)

    @pl.loop(0, TROWS // 4, unroll=4)
    def _(k):
        f = jnp.maximum(dot(v2c[...], nine_taps(fs, k * 4, 4)) + v2b_col, 0.0)
        inv = inv_norm(f)
        u = f * inv
        diff = u - unit_t[:, span(k * 512, 512, 128)]
        weighted = lin_col * diff
        loss_acc[...] += jnp.sum(weighted * diff, axis=0, keepdims=True)
        g = weighted * (2.0 * LOSS_SCALE / PIX)
        g = inv * (g - u * jnp.sum(g * u, axis=0, keepdims=True))
        shift_store(gs, jnp.where(f > 0.0, g, 0.0), k * 4, 4)

    loss = jnp.sum(loss_acc[...], axis=1, keepdims=True) * (1.0 / PIX)
    grads[REST + 96 : REST + 104, :] = jnp.broadcast_to(loss, (8, 128))
    grads[18 * CH + 104 :, :] = jnp.zeros((GRAD_ROWS - 18 * CH - 104, CH), F32)
    for p in range(3):
        line_sum[p, SHARE:] = jnp.zeros((128 - SHARE, CH), F32)

    v1_back = jnp.concatenate(
        [
            v1f[(2 - a) * 32 + (2 - b) * 8 : (2 - a) * 32 + (2 - b) * 8 + 8, :]
            for b in range(3)
            for a in range(3)
        ],
        axis=0,
    ).astype(BF)

    @pl.loop(0, TROWS // 4, unroll=4)
    def _(k):
        g = dot(v2t[...], nine_taps(gs, k * 4, 4)).astype(BF)
        at = span((k * 4 + 1) * 128, 512, 128)
        g = jnp.where(fs[1, :, at] > 0, g, jnp.zeros_like(g))
        y_ref[:, at] = dot(v1_back, g)

    def table_adjoint(k, acc):
        at = span(k * 1024, 1024, 128)
        part = []
        for b in range(3):
            part.append(
                sum(
                    y_ref[(b * 3 + a) * 8 : (b * 3 + a) * 8 + 8, span((k * 8 + a) * 128, 1024, 128)]
                    for a in range(3)
                )
            )
        col = jnp.bitwise_and(lax.broadcasted_iota(jnp.int32, (8, 1024), 1), 127)
        dz = (
            jnp.where(col > 0, pltpu.roll(part[0], 1, 1), 0.0)
            + part[1]
            + jnp.where(col < 127, pltpu.roll(part[2], 1023, 1), 0.0)
        )
        dz = dz.astype(BF).astype(F32) / per_channel(SPREAD)
        spread = jnp.concatenate(
            [w[:, at] * dz[c : c + 1] for w in (al, ar) for c in range(3)], axis=0
        )
        hi = spread.astype(BF)
        lo = (spread - hi.astype(F32)).astype(BF)
        return acc + dot(jnp.concatenate([hi, lo], axis=0), hot[:, at], 1, 1)

    acc = lax.fori_loop(0, 8, table_adjoint, jnp.zeros((96, 384), F32), unroll=4)
    acc = acc[0:48] + acc[48:96]
    adjoint = acc[0:24] + pltpu.roll(acc[24:48], 1, 1)
    for k in range(3):
        for c in range(3):
            tb[k, c] = adjoint[c * 8 : c * 8 + 8, k * 128 : (k + 1) * 128]
    pb[1, :, 8:16, :] = tb[1]

    returned = []
    for i, (k, dl) in enumerate(((0, -1), (2, 1))):
        copy = pltpu.make_async_remote_copy(
            src_ref=tb.at[k],
            dst_ref=pb.at[k, :, pl.ds(8, 8), :],
            send_sem=tab_send.at[i],
            recv_sem=tab_recv.at[i],
            device_id=near(dl, 0),
            device_id_type=MESH,
        )
        copy.start()
        returned.append(copy)
    def turn(act, turned, first_row):
        @pl.loop(0, ROWS + 2, unroll=3)
        def _(r):
            block = act[r + first_row].astype(F32).T
            at = span(r * 128, 128, 128)
            for b in range(3):
                turned[b, :, at] = block[:, 15 + b : 15 + b + COLS].astype(BF)

    turn(a1, t1, 1)
    for copy in returned:
        copy.wait()

    for c in range(3):
        placed = sum(pb[k, c, pl.ds(8 - rows_ref[k, 0, 0], ROWS), :] for k in range(3))
        ca[c] = placed.astype(BF)

    exchanged = []
    for i, (dl, dg) in enumerate(AROUND):
        copy = pltpu.make_async_remote_copy(
            src_ref=ca,
            dst_ref=ca_near.at[7 - i],
            send_sem=adj_send.at[i],
            recv_sem=adj_recv.at[7 - i],
            device_id=near(dl, dg),
            device_id_type=MESH,
        )
        copy.start()
        exchanged.append(copy)

    def taps_of(target_e, c, field):
        for b in range(3):
            moved = pltpu.roll(field, 384 - (111 + 2 - b), 1)[:, 0:256]
            target_e[:, b * 8 + c, :] = moved

    def patches(source_e, r):
        return jnp.concatenate([source_e[r + a] for a in range(3)], axis=0)[:, :WIDE].astype(BF)

    rows2 = jnp.zeros((2, 384), F32)
    own = [ca[c].astype(F32) for c in range(3)]
    for c in range(3):
        side = jnp.zeros((ROWS, 128), F32)
        middle = jnp.concatenate([side, own[c], side], axis=1)
        taps_of(own_e, c, jnp.concatenate([rows2, middle, rows2], axis=0))
    grad_out = jnp.zeros((96, CH), F32)
    for r in range(ROWS + 2):
        grad_out += dot(patches(own_e, r), a2[r])
    for a in range(3):
        base = REST + (2 - a) * 32
        grads[base : base + 32, :] = grad_out[a * 32 : a * 32 + 32]

    turn(a0, t0, 2)
    for copy in exchanged:
        copy.wait()
    at_of = {delta: i for i, delta in enumerate(AROUND)}
    has_north = jnp.where(north, 0.0, 1.0)
    has_south = jnp.where(south, 0.0, 1.0)
    for c in range(3):

        def line(dg):
            parts = [
                own[c] if (dl, dg) == (0, 0) else ca_near[at_of[(dl, dg)], c].astype(F32)
                for dl in (-1, 0, 1)
            ]
            return jnp.concatenate(parts, axis=1)

        field = jnp.concatenate(
            [line(-1)[ROWS - 2 :] * has_north, line(0), line(1)[0:2] * has_south], axis=0
        )
        taps_of(all_e, c, field)

    wo_flip = jnp.concatenate([wof[2 - a] for a in range(3)], axis=0).astype(BF)
    for r in range(ROWS + 2):
        d2[r] = (dot(patches(all_e, r), wo_flip, 0, 0) * s2[r]).astype(BF)
    clear(d2, 1)

    def weight_grad(turned, adj, base, taps):
        for a in taps:
            at = base + a * 3 * CH
            shifted = [turned[b, :, a * 128 : a * 128 + ROWS * 128] for b in range(3)]
            grads[at : at + 3 * CH, :] = dot(jnp.concatenate(shifted, axis=0), adj)

    weight_grad(t1, d2[1 : 1 + ROWS, 16 : 16 + COLS, :].reshape(ROWS * COLS, CH), 0, range(3))
    first = scatter_part(0, grads, line_in, sum_sems)

    @pl.loop(0, 4, unroll=4)
    def _(k):
        r = k * 4
        g = conv_rows(d2, w2f[...], r, 4, 1) * s1[pl.ds(r + 2, 4)].reshape(4 * WIDE, CH)
        d1[pl.ds(r, 4)] = g.reshape(4, WIDE, CH)[:, 16 : 16 + COLS].astype(BF)

    d1_all = d1[...].reshape(ROWS * COLS, CH)
    weight_grad(t0, d1_all, ONE, range(0, 2))
    first += scatter_part(1, grads, line_in, sum_sems)
    weight_grad(t0, d1_all, ONE, range(2, 3))
    first += scatter_part(2, grads, line_in, sum_sems)

    sum_all(first, grads, total, line_in, line_sum, plane_in, plane_sum, gathered, sum_sems)
    outs = []
    for i, (out, at, size) in enumerate(
        ((one_out, ONE, 9 * CH), (two_out, 0, 9 * CH), (rest_out, REST, 104))
    ):
        copy = pltpu.make_async_copy(total.at[at : at + size], out, out_sem.at[i])
        copy.start()
        outs.append(copy)
    for copy in outs:
        copy.wait()


def run_kernel(*args):
    vmem = pl.BlockSpec(memory_space=pltpu.VMEM)
    smem = pl.BlockSpec(memory_space=pltpu.SMEM)
    specs = [vmem] * 16
    specs[6] = smem
    specs[12] = smem
    dma = pltpu.SemaphoreType.DMA
    return pl.pallas_call(
        kernel,
        out_shape=(
            jax.ShapeDtypeStruct((9 * CH, CH), F32),
            jax.ShapeDtypeStruct((9 * CH, CH), F32),
            jax.ShapeDtypeStruct((104, CH), F32),
        ),
        in_specs=specs,
        out_specs=(pl.BlockSpec(memory_space=pl.ANY),) * 3,
        scratch_shapes=[
            pltpu.VMEM((ROWS + 6, WIDE, CH), BF),
            pltpu.VMEM((ROWS + 6, WIDE, CH), BF),
            pltpu.VMEM((ROWS + 4, WIDE, CH), BF),
            pltpu.VMEM((ROWS + 2, WIDE, CH), BF),
            pltpu.VMEM((ROWS + 4, WIDE, CH), F32),
            pltpu.VMEM((ROWS + 2, WIDE, CH), F32),
            pltpu.VMEM((3 * CH, 3 * CH), BF),
            pltpu.VMEM((3 * CH, 3 * CH), BF),
            pltpu.VMEM((3 * CH, 3 * CH), BF),
            pltpu.VMEM((3, ROWS, COLS), F32),
            pltpu.VMEM((2, 3, ROWS, COLS), F32),
            pltpu.VMEM((384, PIX), BF),
            pltpu.VMEM((8, PIX), F32),
            pltpu.VMEM((8, PIX), F32),
            pltpu.VMEM((96, VW), F32),
            pltpu.VMEM((VW, 9 * VW), BF),
            pltpu.VMEM((VW, 9 * VW), BF),
            pltpu.VMEM((32, PIX + 256), BF),
            pltpu.VMEM((3, VW, PIX + 256), BF),
            pltpu.VMEM((3, VW, PIX + 256), BF),
            pltpu.VMEM((VW, PIX), F32),
            pltpu.VMEM((72, PIX + 256), F32),
            pltpu.VMEM((3, 3, 8, 128), F32),
            pltpu.VMEM((3, 3, 24, 128), F32),
            pltpu.VMEM((3, ROWS, COLS), BF),
            pltpu.VMEM((8, 3, ROWS, COLS), BF),
            pltpu.VMEM((ROWS + 4, 32, 256), F32),
            pltpu.VMEM((ROWS + 4, 32, 256), F32),
            pltpu.VMEM((ROWS + 2, WIDE, CH), BF),
            pltpu.VMEM((ROWS, COLS, CH), BF),
            pltpu.VMEM((3, CH, (ROWS + 2) * COLS), BF),
            pltpu.VMEM((3, CH, (ROWS + 2) * COLS), BF),
            pltpu.VMEM((1, 512), F32),
            pltpu.VMEM((3, 32, CH), F32),
            pltpu.VMEM((2, ROWS * 8, CH), BF),
            pltpu.VMEM((2, ROWS * 8, CH), BF),
            pltpu.VMEM((GRAD_ROWS, CH), F32),
            pltpu.VMEM((GRAD_ROWS, CH), F32),
            pltpu.VMEM((3, 7, SHARE, CH), F32),
            pltpu.VMEM((3, 128, CH), F32),
            pltpu.VMEM((3, 15, 8, CH), F32),
            pltpu.VMEM((3, 8, CH), F32),
            pltpu.VMEM((3, 128, CH), F32),
            dma((8,)), dma((8,)), dma((2,)), dma((2,)), dma((2,)), dma((2,)), dma((8,)), dma((8,)), dma((3,)),
            dma((3,)), dma((3,)), dma((3,)), dma((3,)), dma((3,)), dma((3,)), dma((3,)), dma((3,)),
        ],
        compiler_params=pltpu.CompilerParams(
            collective_id=0, has_side_effects=True, vmem_limit_bytes=56 * 1024 * 1024
        ),
    )(*args)


def hand_over_kernel(one, two, rest, loss, one_out, two_out, grad_out, sems):
    copies = []
    for i, (src, dst) in enumerate(((one, one_out), (two, two_out))):
        copy = pltpu.make_async_copy(src, dst, sems.at[i])
        copy.start()
        copies.append(copy)
    for a in range(3):
        for b in range(3):
            grad_out[a, b] = rest[a * 32 + b * 8 : a * 32 + b * 8 + 3, :]
    loss[...] = rest[96:97, 0:1]
    for copy in copies:
        copy.wait()


def hand_over(one, two, rest):
    vmem, hbm = pl.BlockSpec(memory_space=pltpu.VMEM), pl.BlockSpec(memory_space=pl.ANY)
    block = jax.ShapeDtypeStruct((9 * CH, CH), F32)
    return pl.pallas_call(
        hand_over_kernel,
        out_shape=(
            jax.ShapeDtypeStruct((1, 1), F32),
            block,
            block,
            jax.ShapeDtypeStruct((3, 3, 3, CH), F32),
        ),
        in_specs=[vmem, vmem, vmem],
        out_specs=(vmem, hbm, hbm, vmem),
        scratch_shapes=[pltpu.SemaphoreType.DMA((2,))],
    )(one, two, rest)


def per_device(
    features,
    conv_one_w,
    conv_one_b,
    conv_two_w,
    conv_two_b,
    out_conv_w,
    out_conv_b,
    vgg_one_w,
    vgg_one_b,
    vgg_two_w,
    vgg_two_b,
    lin_weights,
    row_lists,
    tap_index,
    tap_weight,
    target_tiles,
):
    grad_one, grad_two, rest = run_kernel(
        features,
        conv_one_w,
        conv_one_b.reshape(1, CH),
        conv_two_w,
        conv_two_b.reshape(1, CH),
        jnp.transpose(out_conv_w, (0, 1, 3, 2)),
        out_conv_b,
        jnp.transpose(vgg_one_w, (1, 2, 3, 0)),
        vgg_one_b.reshape(1, VW),
        jnp.transpose(vgg_two_w, (2, 3, 0, 1)),
        vgg_two_b.reshape(1, VW),
        lin_weights.reshape(1, VW),
        jnp.transpose(row_lists, (1, 0, 2)),
        tap_index[0],
        tap_weight[0],
        target_tiles[0],
    )
    loss, grad_one, grad_two, grad_out = hand_over(grad_one, grad_two, rest)
    return (
        loss.reshape(()),
        grad_one.reshape(3, 3, CH, CH),
        grad_two.reshape(3, 3, CH, CH),
        jnp.transpose(grad_out, (0, 1, 3, 2)),
    )


def solution(mesh):
    in_specs = (
        P("grp", "lon", None),
        P(),
        P(),
        P(),
        P(),
        P(),
        P(),
        P(),
        P(),
        P(),
        P(),
        P(),
        P(("lon", "grp"), None, None),
        P(("lon", "grp"), None, None),
        P(("lon", "grp"), None, None),
        P(("lon", "grp"), None, None, None),
    )
    out_specs = (P(), P(), P(), P())
    return jax.shard_map(
        per_device, mesh=mesh, in_specs=in_specs, out_specs=out_specs, check_vma=False
    )
```

```python
import jax
import jax.numpy as jnp
from jax import lax
from jax.experimental import pallas as pl
from jax.experimental.pallas import tpu as pltpu
from jax.sharding import PartitionSpec as P

OFFSET = (-0.03, -0.088, -0.188)
SPREAD = (0.458, 0.448, 0.45)
LOSS_SCALE = 64.0

CH = 128
VW = 64
ROWS = 16
COLS = 128
WIDE = 160
TROWS = 64
PIX = TROWS * 128
BF = jnp.bfloat16
F32 = jnp.float32
MESH = pl.DeviceIdType.MESH

AROUND = ((-1, -1), (-1, 0), (-1, 1), (0, -1), (0, 1), (1, -1), (1, 0), (1, 1))


PARTS = ((0, (1, 2)), (1, (0, 2)), (2, (0, 1)))
GRAD_ROWS = 2496
REST = 9 * CH
ONE = 9 * CH + 104
PART = GRAD_ROWS // 3
SHARE = PART // 8
LINE_STEPS = [(d, k) for d in range(4) for k in range(2) if (d, k) != (0, 0)]
PLANE_STEPS = [(d, e) for d in range(4) for e in range(4) if (d, e) != (0, 0)]


def place():
    lon, grp = lax.axis_index("lon"), lax.axis_index("grp")
    return (lon // 8, (lon % 2) * 2 + grp // 2, (lon // 2) % 4), grp % 2


def device(xyz, core):
    x, y, z = xyz
    return ((x * 4 + z) * 2 + y // 2, (y % 2) * 2 + core)


def line_peers(axis):
    xyz, core = place()
    for d, k in LINE_STEPS:
        at, its_core = (xyz[axis] + d) % 4, (core + k) % 2
        peer = tuple(at if i == axis else xyz[i] for i in range(3))
        yield device(peer, its_core), at * 2 + its_core


def plane_peers(axes):
    xyz, core = place()
    u, v = axes
    for d, e in PLANE_STEPS:
        at_u, at_v = (xyz[u] + d) % 4, (xyz[v] + e) % 4
        peer = tuple(at_u if i == u else at_v if i == v else xyz[i] for i in range(3))
        yield device(peer, core), at_u * 4 + at_v


def sum_offsets():
    found = set()
    for axis, axes in PARTS:
        for d, k in LINE_STEPS:
            found.add(tuple(d if i == axis else 0 for i in range(3)) + (k,))
        for d, e in PLANE_STEPS:
            found.add(tuple(d if i == axes[0] else e if i == axes[1] else 0 for i in range(3)) + (0,))
    return sorted(found)


def rows8(start, size):
    return pl.ds(pl.multiple_of(start, 8), size)


def send(src, dst, send_sem, recv_sem, to):
    copy = pltpu.make_async_remote_copy(
        src_ref=src, dst_ref=dst, send_sem=send_sem, recv_sem=recv_sem, device_id=to, device_id_type=MESH
    )
    copy.start()
    return copy


def scatter_part(p, grads, line_in, sems):
    copies = []
    for i, (peer, index) in enumerate(line_peers(PARTS[p][0])):
        src = grads.at[rows8(p * PART + index * SHARE, SHARE)]
        copies.append(send(src, line_in.at[p, i], sems[0].at[p], sems[1].at[p], peer))
    return copies


def sum_all(first, grads, out, line_in, line_sum, plane_in, plane_sum, gathered, sems):
    ls, lr, ps, pr, gs, gr, os, orr = sems

    def all_of(ref, sem):
        pltpu.make_async_copy(ref, ref, sem).wait()

    xyz, core = place()
    second = []
    for p, (axis, axes) in enumerate(PARTS):
        mine = xyz[axis] * 2 + core
        all_of(line_in.at[p], lr.at[p])
        total = grads[rows8(p * PART + mine * SHARE, SHARE), :]
        for i in range(7):
            total = total + line_in[p, i]
        line_sum[p, 0:SHARE] = total
        for i, (peer, index) in enumerate(plane_peers(axes)):
            src = line_sum.at[p, rows8(index * 8, 8)]
            second.append(send(src, plane_in.at[p, i], ps.at[p], pr.at[p], peer))
    third = []
    for p, (axis, axes) in enumerate(PARTS):
        mine = xyz[axes[0]] * 4 + xyz[axes[1]]
        all_of(plane_in.at[p], pr.at[p])
        total = line_sum[p, rows8(mine * 8, 8), :]
        for i in range(15):
            total = total + plane_in[p, i]
        plane_sum[p] = total
        gathered[p, rows8(mine * 8, 8), :] = total
        for i, (peer, index) in enumerate(plane_peers(axes)):
            dst = gathered.at[p, rows8(mine * 8, 8)]
            third.append(send(plane_sum.at[p], dst, gs.at[p], gr.at[p], peer))
    fourth = []
    for p, (axis, axes) in enumerate(PARTS):
        mine = xyz[axis] * 2 + core
        at = rows8(p * PART + mine * SHARE, SHARE)
        all_of(gathered.at[p, 0:120], gr.at[p])
        for i, (peer, index) in enumerate(line_peers(axis)):
            fourth.append(send(gathered.at[p, 0:SHARE], out.at[at], os.at[p], orr.at[p], peer))
        out[at, :] = gathered[p, 0:SHARE]
    for p in range(3):
        all_of(line_in.at[p], ls.at[p])
        all_of(plane_in.at[p], ps.at[p])
        all_of(gathered.at[p, 0:120], gs.at[p])
    for p in range(3):
        all_of(out.at[0 : 7 * SHARE], os.at[p])
        all_of(out.at[0 : 7 * SHARE], orr.at[p])


HALO_ORDER = (1, 6, 3, 4, 0, 2, 5, 7)


def dot(a, b, ca=1, cb=0):
    return lax.dot_general(a, b, (((ca,), (cb,)), ((), ())), preferred_element_type=F32)


def span(start, size, unit):
    if isinstance(start, int):
        return pl.ds(start, size)
    return pl.ds(pl.multiple_of(start, unit), size)


def ext(delta, low, high):
    return low if delta < 0 else high


def conv_rows(src, weight, r, n, last=0):
    lhs = jnp.concatenate(
        [src[pl.ds(r + a, n)].reshape(n * WIDE, CH) for a in range(3)], axis=1
    )
    z = dot(lhs, weight, 1, last)
    return (
        pltpu.roll(z[:, :CH], 1, 0)
        + z[:, CH : 2 * CH]
        + pltpu.roll(z[:, 2 * CH :], n * WIDE - 1, 0)
    )


def act_slope(hidden):
    h = hidden.astype(F32)
    s = jax.nn.sigmoid(h)
    return (h * s).astype(BF), s * (1.0 + h * (1.0 - s))


def lane_masks(n):
    col = lax.broadcasted_iota(jnp.int32, (1, 128), 1)
    return col > 0, col < 127


def shift_store(ref, y, row0, n):
    first, last = lane_masks(n)
    for r in range(n):
        part = y[:, r * 128 : (r + 1) * 128]
        at = span((row0 + r + 1) * 128, 128, 128)
        ref[0, :, at] = jnp.where(first, pltpu.roll(part, 1, 1), 0.0).astype(BF)
        ref[1, :, at] = part.astype(BF)
        ref[2, :, at] = jnp.where(last, pltpu.roll(part, 127, 1), 0.0).astype(BF)


def per_channel(values):
    row = lax.broadcasted_iota(jnp.int32, (8, 1), 0)
    out = jnp.full((8, 1), values[2], F32)
    out = jnp.where(row == 0, values[0], out)
    return jnp.where(row == 1, values[1], out)


def store_scaled(zs, colours, row0, n):
    row = lax.broadcasted_iota(jnp.int32, (8, 1), 0)
    z = jnp.where(row < 3, (colours - per_channel(OFFSET)) / per_channel(SPREAD), 0.0)
    first, last = lane_masks(n)
    for r in range(n):
        part = z[:, r * 128 : (r + 1) * 128]
        stack = jnp.concatenate(
            [
                jnp.where(first, pltpu.roll(part, 1, 1), 0.0),
                part,
                jnp.where(last, pltpu.roll(part, 127, 1), 0.0),
                jnp.zeros_like(part),
            ],
            axis=0,
        )
        zs[:, span((row0 + r + 1) * 128, 128, 128)] = stack.astype(BF)


def vgg_first(zs, fs, v1, v1b, n):
    @pl.loop(0, TROWS // n, unroll=8)
    def _(k):
        r0 = k * n
        rhs = jnp.concatenate(
            [zs[:, span((r0 + a) * 128, n * 128, 128)] for a in range(3)], axis=0
        )
        y = jnp.maximum(dot(v1, rhs) + v1b, 0.0)
        shift_store(fs, y, r0, n)


def nine_taps(ref, r0, n):
    return jnp.concatenate(
        [ref[b, :, span((r0 + a) * 128, n * 128, 128)] for a in range(3) for b in range(3)], axis=0
    )


def inv_norm(f):
    return lax.rsqrt(jnp.sum(f * f, axis=0, keepdims=True) + 1e-05)


def kernel(
    feat, w1, b1, w2, b2, wo, bo, v1w, v1b, v2w, v2b, lin, rows_ref, tap_i, tap_w, target,
    one_out, two_out, rest_out,
    f_ref, a0, a1, a2, s1, s2, w1c, w2c, w2f, c_own, c_near, hot, al, ar, v1f, v2c, v2t,
    zs, fs, gs, unit_t, y_ref, tb, pb, ca, ca_near, own_e, all_e, d2, d1, t0, t1, loss_acc, wof,
    side_out, side_in, grads, total, line_in, line_sum, plane_in, plane_sum, gathered,
    halo_send, halo_recv, col_send, col_recv, tab_send, tab_recv, adj_send, adj_recv, out_sem,
    *sum_sems,
):
    lon, grp = lax.axis_index("lon"), lax.axis_index("grp")
    n_lon, n_grp = lax.axis_size("lon"), lax.axis_size("grp")

    def near(dl, dg):
        return (lax.rem(lon + dl + n_lon, n_lon), lax.rem(grp + dg + n_grp, n_grp))

    barrier = pltpu.get_barrier_semaphore()
    for dl, dg in AROUND:
        pl.semaphore_signal(barrier, inc=1, device_id=near(dl, dg), device_id_type=MESH)
    xyz, core = place()
    peers = sum_offsets()
    for off in peers:
        peer = device([(xyz[i] + off[i]) % 4 for i in range(3)], (core + off[3]) % 2)
        pl.semaphore_signal(barrier, inc=1, device_id=peer, device_id_type=MESH)

    @pl.loop(0, 8, unroll=8)
    def _(k):
        at = span(k * 1024, 1024, 128)
        index = tap_i[:, at]
        weight = tap_w[:, at]
        column = lax.shift_left(lax.shift_right_logical(index, 10), 7) + jnp.bitwise_and(index, 127)
        slot = jnp.bitwise_and(lax.shift_right_logical(index, 7), 7)
        left = jnp.min(column, axis=0, keepdims=True)
        top = jnp.min(slot, axis=0, keepdims=True)
        is_left, is_top = column == left, slot == top

        def corner(cond):
            return jnp.sum(jnp.where(cond, weight, 0.0), axis=0, keepdims=True)

        not_left, not_top = jnp.logical_not(is_left), jnp.logical_not(is_top)
        w_tl, w_tr = corner(is_top & is_left), corner(is_top & not_left)
        w_bl, w_br = corner(not_top & is_left), corner(not_top & not_left)
        j = lax.broadcasted_iota(jnp.int32, (8, 1024), 0)
        on_top, on_next = j == top, j == top + 1
        al[:, at] = jnp.where(on_top, w_tl, jnp.where(on_next, w_bl, 0.0))
        ar[:, at] = jnp.where(on_top, w_tr, jnp.where(on_next, w_br, 0.0))
        x = lax.broadcasted_iota(jnp.int32, (384, 1024), 0)
        hot[:, at] = jnp.where(x == left, 1.0, 0.0).astype(BF)

    side_out[0] = feat[:, 0:8, :].astype(F32).reshape(ROWS * 8, CH).astype(BF)
    side_out[1] = feat[:, COLS - 8 :, :].astype(F32).reshape(ROWS * 8, CH).astype(BF)
    pl.semaphore_wait(barrier, len(AROUND) + len(peers))
    take_r = {-1: pl.ds(0, 3), 1: pl.ds(ROWS - 3, 3)}
    take_c = {-1: pl.ds(0, 16), 0: pl.ds(0, COLS), 1: pl.ds(COLS - 16, 16)}
    land_r = {-1: pl.ds(ROWS + 3, 3), 1: pl.ds(0, 3)}
    land_c = {-1: pl.ds(COLS + 16, 16), 0: pl.ds(16, COLS), 1: pl.ds(0, 16)}
    north, south = grp == 0, grp == n_grp - 1
    sends = {-1: grp > 0, 0: None, 1: grp < n_grp - 1}
    lands = {-1: sends[1], 0: None, 1: sends[-1]}

    def only_if(cond, act):
        if cond is None:
            act()
        else:
            pl.when(cond)(act)

    halo = []
    for i in HALO_ORDER:
        dl, dg = AROUND[i]
        if dg == 0:
            src, dst = side_out.at[(1 + dl) // 2], side_in.at[(1 + dl) // 2]
        else:
            src = feat.at[take_r[dg], take_c[dl]]
            dst = f_ref.at[land_r[dg], land_c[dl]]
        copy = pltpu.make_async_remote_copy(
            src_ref=src,
            dst_ref=dst,
            send_sem=halo_send.at[i],
            recv_sem=halo_recv.at[i],
            device_id=near(dl, dg),
            device_id_type=MESH,
        )
        only_if(sends[dg], copy.start)
        halo.append((dg, copy))
    f_ref[3 : 3 + ROWS, 16 : 16 + COLS, :] = feat[...]

    for a in range(3):
        for b in range(3):
            rows, cols = slice(a * CH, (a + 1) * CH), slice(b * CH, (b + 1) * CH)
            w1c[rows, cols] = w1[a, b]
            w2c[rows, cols] = w2[a, b]
            w2f[cols, rows] = w2[2 - a, 2 - b]
    v1f[...] = jnp.zeros_like(v1f)
    wof[...] = jnp.zeros_like(wof)
    for a in range(3):
        for b in range(3):
            for c in range(3):
                v1f[a * 32 + b * 8 + c : a * 32 + b * 8 + c + 1, :] = v1w[c, a, b : b + 1].astype(F32)
            wof[a, b * 8 : b * 8 + 3, :] = wo[a, b].astype(F32)
            v2c[:, (a * 3 + b) * VW : (a * 3 + b + 1) * VW] = v2w[a, b]
            v2t[:, (a * 3 + b) * VW : (a * 3 + b + 1) * VW] = (
                v2w[2 - a, 2 - b].astype(F32).T.astype(BF)
            )
    v1 = v1f[...].T.astype(BF)
    v1b_col = v1b[...].reshape(VW, 1)
    v2b_col = v2b[...].reshape(VW, 1)
    lin_col = lin[...].reshape(VW, 1)

    zs[:, 0:128] = jnp.zeros((32, 128), BF)
    zs[:, PIX + 128 :] = jnp.zeros((32, 128), BF)
    for ref in (fs, gs):
        ref[:, :, 0:128] = jnp.zeros((3, VW, 128), BF)
        ref[:, :, PIX + 128 :] = jnp.zeros((3, VW, 128), BF)
    y_ref[:, 0:128] = jnp.zeros((72, 128), F32)
    y_ref[:, PIX + 128 :] = jnp.zeros((72, 128), F32)
    pb[:, :, 0:8, :] = jnp.zeros((3, 3, 8, 128), F32)
    pb[:, :, 16:24, :] = jnp.zeros((3, 3, 8, 128), F32)
    own_e[...] = jnp.zeros_like(own_e)
    all_e[...] = jnp.zeros_like(all_e)

    for r in range(TROWS):
        tgt = target[:, r, :].astype(F32)
        unit_t[0:8, r * 128 : (r + 1) * 128] = jnp.concatenate(
            [tgt, jnp.zeros((5, 128), F32)], axis=0
        )

    @pl.loop(0, 8, unroll=8)
    def _(k):
        store_scaled(zs, unit_t[0:8, span(k * 1024, 1024, 128)], k * 8, 8)

    vgg_first(zs, fs, v1, v1b_col, 4)

    a0[3 : 3 + ROWS, 16 : 16 + COLS, :] = act_slope(feat[...])[0]
    for dg, copy in halo:
        only_if(sends[dg], copy.wait_send)
        only_if(lands[dg], copy.wait_recv)
    blank = jnp.zeros((ROWS, 8, CH), F32)
    west = side_in[1].astype(F32).reshape(ROWS, 8, CH)
    east = side_in[0].astype(F32).reshape(ROWS, 8, CH)
    f_ref[3 : 3 + ROWS, 0:16, :] = jnp.concatenate([blank, west], axis=1).astype(BF)
    f_ref[3 : 3 + ROWS, 16 + COLS :, :] = jnp.concatenate([east, blank], axis=1).astype(BF)
    for rows, cols in (
        (slice(0, 3), slice(0, WIDE)),
        (slice(ROWS + 3, ROWS + 6), slice(0, WIDE)),
        (slice(3, ROWS + 3), slice(0, 16)),
        (slice(3, ROWS + 3), slice(16 + COLS, WIDE)),
    ):
        a0[rows, cols, :] = act_slope(f_ref[rows, cols, :])[0]

    def clear(ref, rows):
        @pl.when(north)
        def _():
            ref[0:rows] = jnp.zeros((rows, WIDE, CH), BF)

        @pl.when(south)
        def _():
            ref[ref.shape[0] - rows :] = jnp.zeros((rows, WIDE, CH), BF)

    clear(a0, 3)

    @pl.loop(0, 5, unroll=5)
    def _(k):
        r = k * 4
        h = (conv_rows(a0, w1c[...], r, 4) + b1[...]).astype(BF)
        act, slope = act_slope(h)
        a1[pl.ds(r, 4)] = act.reshape(4, WIDE, CH)
        s1[pl.ds(r, 4)] = slope.reshape(4, WIDE, CH)

    clear(a1, 2)

    @pl.loop(0, 6, unroll=6)
    def _(k):
        r = k * 3
        f = f_ref[pl.ds(r + 2, 3)].reshape(3 * WIDE, CH).astype(F32)
        h = (f + conv_rows(a1, w2c[...], r, 3) + b2[...]).astype(BF)
        act, slope = act_slope(h)
        a2[pl.ds(r, 3)] = act.reshape(3, WIDE, CH)
        s2[pl.ds(r, 3)] = slope.reshape(3, WIDE, CH)

    clear(a2, 1)

    wo_cat = jnp.concatenate([wof[a] for a in range(3)], axis=1).astype(BF)
    for r in range(ROWS):
        rhs = jnp.concatenate([a2[r + a] for a in range(3)], axis=1)
        z = dot(wo_cat, rhs, 1, 1)
        colour = z[0:8, 15 : 15 + COLS] + z[8:16, 16 : 16 + COLS] + z[16:24, 17 : 17 + COLS]
        for c in range(3):
            c_own[c, r : r + 1, :] = colour[c : c + 1] + bo[c]

    colours = []
    for i, dl in enumerate((-1, 1)):
        copy = pltpu.make_async_remote_copy(
            src_ref=c_own,
            dst_ref=c_near.at[1 - i],
            send_sem=col_send.at[i],
            recv_sem=col_recv.at[1 - i],
            device_id=near(dl, 0),
            device_id_type=MESH,
        )
        copy.start()
        colours.append(copy)

    @pl.loop(0, TROWS // 4, unroll=8)
    def _(k):
        f = jnp.maximum(dot(v2c[...], nine_taps(fs, k * 4, 4)) + v2b_col, 0.0)
        unit_t[:, span(k * 512, 512, 128)] = f * inv_norm(f)

    for copy in colours:
        copy.wait()

    start = rows_ref[1, 0, 0]
    slabs = (c_near.at[0], c_own, c_near.at[1])
    table = jnp.concatenate(
        [
            jnp.concatenate([slab[c, pl.ds(start, 8), :] for c in range(3)], axis=0)
            for slab in slabs
        ],
        axis=1,
    )
    table = jnp.concatenate([table, pltpu.roll(table, 383, 1)], axis=0)
    table_hi = table.astype(BF)
    table_lo = (table - table_hi.astype(F32)).astype(BF)
    table = jnp.concatenate([table_hi, table_lo], axis=0)

    @pl.loop(0, 8, unroll=8)
    def _(k):
        at = span(k * 1024, 1024, 128)
        got = dot(table, hot[:, at])
        got = got[0:48] + got[48:96]
        w_left, w_right = al[:, at], ar[:, at]
        picture = [
            jnp.sum(
                got[c * 8 : c * 8 + 8] * w_left + got[24 + c * 8 : 32 + c * 8] * w_right,
                axis=0,
                keepdims=True,
            )
            for c in range(3)
        ]
        picture = jnp.concatenate(picture + [jnp.zeros((5, 1024), F32)], axis=0)
        store_scaled(zs, picture, k * 8, 8)

    vgg_first(zs, fs, v1, v1b_col, 4)
    loss_acc[...] = jnp.zeros_like(loss_acc)

    @pl.loop(0, TROWS // 4, unroll=8)
    def _(k):
        f = jnp.maximum(dot(v2c[...], nine_taps(fs, k * 4, 4)) + v2b_col, 0.0)
        inv = inv_norm(f)
        u = f * inv
        diff = u - unit_t[:, span(k * 512, 512, 128)]
        weighted = lin_col * diff
        loss_acc[...] += jnp.sum(weighted * diff, axis=0, keepdims=True)
        g = weighted * (2.0 * LOSS_SCALE / PIX)
        g = inv * (g - u * jnp.sum(g * u, axis=0, keepdims=True))
        shift_store(gs, jnp.where(f > 0.0, g, 0.0), k * 4, 4)

    loss = jnp.sum(loss_acc[...], axis=1, keepdims=True) * (1.0 / PIX)
    grads[REST + 96 : REST + 104, :] = jnp.broadcast_to(loss, (8, 128))
    grads[18 * CH + 104 :, :] = jnp.zeros((GRAD_ROWS - 18 * CH - 104, CH), F32)
    for p in range(3):
        line_sum[p, SHARE:] = jnp.zeros((128 - SHARE, CH), F32)

    v1_back = jnp.concatenate(
        [
            v1f[(2 - a) * 32 + (2 - b) * 8 : (2 - a) * 32 + (2 - b) * 8 + 8, :]
            for b in range(3)
            for a in range(3)
        ],
        axis=0,
    ).astype(BF)

    @pl.loop(0, TROWS // 4, unroll=8)
    def _(k):
        g = dot(v2t[...], nine_taps(gs, k * 4, 4)).astype(BF)
        at = span((k * 4 + 1) * 128, 512, 128)
        g = jnp.where(fs[1, :, at] > 0, g, jnp.zeros_like(g))
        y_ref[:, at] = dot(v1_back, g)

    def table_adjoint(k, acc):
        at = span(k * 1024, 1024, 128)
        part = []
        for b in range(3):
            part.append(
                sum(
                    y_ref[(b * 3 + a) * 8 : (b * 3 + a) * 8 + 8, span((k * 8 + a) * 128, 1024, 128)]
                    for a in range(3)
                )
            )
        col = jnp.bitwise_and(lax.broadcasted_iota(jnp.int32, (8, 1024), 1), 127)
        dz = (
            jnp.where(col > 0, pltpu.roll(part[0], 1, 1), 0.0)
            + part[1]
            + jnp.where(col < 127, pltpu.roll(part[2], 1023, 1), 0.0)
        )
        dz = dz.astype(BF).astype(F32) / per_channel(SPREAD)
        spread = jnp.concatenate(
            [w[:, at] * dz[c : c + 1] for w in (al, ar) for c in range(3)], axis=0
        )
        hi = spread.astype(BF)
        lo = (spread - hi.astype(F32)).astype(BF)
        return acc + dot(jnp.concatenate([hi, lo], axis=0), hot[:, at], 1, 1)

    acc = lax.fori_loop(0, 8, table_adjoint, jnp.zeros((96, 384), F32), unroll=8)
    acc = acc[0:48] + acc[48:96]
    adjoint = acc[0:24] + pltpu.roll(acc[24:48], 1, 1)
    for k in range(3):
        for c in range(3):
            tb[k, c] = adjoint[c * 8 : c * 8 + 8, k * 128 : (k + 1) * 128]
    pb[1, :, 8:16, :] = tb[1]

    returned = []
    for i, (k, dl) in enumerate(((0, -1), (2, 1))):
        copy = pltpu.make_async_remote_copy(
            src_ref=tb.at[k],
            dst_ref=pb.at[k, :, pl.ds(8, 8), :],
            send_sem=tab_send.at[i],
            recv_sem=tab_recv.at[i],
            device_id=near(dl, 0),
            device_id_type=MESH,
        )
        copy.start()
        returned.append(copy)
    def turn(act, turned, first_row):
        @pl.loop(0, ROWS + 2, unroll=3)
        def _(r):
            block = act[r + first_row].astype(F32).T
            at = span(r * 128, 128, 128)
            for b in range(3):
                turned[b, :, at] = block[:, 15 + b : 15 + b + COLS].astype(BF)

    turn(a1, t1, 1)
    for copy in returned:
        copy.wait()

    for c in range(3):
        placed = sum(pb[k, c, pl.ds(8 - rows_ref[k, 0, 0], ROWS), :] for k in range(3))
        ca[c] = placed.astype(BF)

    exchanged = []
    for i, (dl, dg) in enumerate(AROUND):
        copy = pltpu.make_async_remote_copy(
            src_ref=ca,
            dst_ref=ca_near.at[7 - i],
            send_sem=adj_send.at[i],
            recv_sem=adj_recv.at[7 - i],
            device_id=near(dl, dg),
            device_id_type=MESH,
        )
        copy.start()
        exchanged.append(copy)

    def taps_of(target_e, c, field):
        for b in range(3):
            moved = pltpu.roll(field, 384 - (111 + 2 - b), 1)[:, 0:256]
            target_e[:, b * 8 + c, :] = moved

    def patches(source_e, r):
        return jnp.concatenate([source_e[r + a] for a in range(3)], axis=0)[:, :WIDE].astype(BF)

    rows2 = jnp.zeros((2, 384), F32)
    own = [ca[c].astype(F32) for c in range(3)]
    for c in range(3):
        side = jnp.zeros((ROWS, 128), F32)
        middle = jnp.concatenate([side, own[c], side], axis=1)
        taps_of(own_e, c, jnp.concatenate([rows2, middle, rows2], axis=0))
    grad_out = jnp.zeros((96, CH), F32)
    for r in range(ROWS + 2):
        grad_out += dot(patches(own_e, r), a2[r])
    for a in range(3):
        base = REST + (2 - a) * 32
        grads[base : base + 32, :] = grad_out[a * 32 : a * 32 + 32]

    turn(a0, t0, 2)
    for copy in exchanged:
        copy.wait()
    at_of = {delta: i for i, delta in enumerate(AROUND)}
    has_north = jnp.where(north, 0.0, 1.0)
    has_south = jnp.where(south, 0.0, 1.0)
    for c in range(3):

        def line(dg):
            parts = [
                own[c] if (dl, dg) == (0, 0) else ca_near[at_of[(dl, dg)], c].astype(F32)
                for dl in (-1, 0, 1)
            ]
            return jnp.concatenate(parts, axis=1)

        field = jnp.concatenate(
            [line(-1)[ROWS - 2 :] * has_north, line(0), line(1)[0:2] * has_south], axis=0
        )
        taps_of(all_e, c, field)

    wo_flip = jnp.concatenate([wof[2 - a] for a in range(3)], axis=0).astype(BF)
    for r in range(ROWS + 2):
        d2[r] = (dot(patches(all_e, r), wo_flip, 0, 0) * s2[r]).astype(BF)
    clear(d2, 1)

    def weight_grad(turned, adj, base, taps):
        for a in taps:
            at = base + a * 3 * CH
            shifted = [turned[b, :, a * 128 : a * 128 + ROWS * 128] for b in range(3)]
            grads[at : at + 3 * CH, :] = dot(jnp.concatenate(shifted, axis=0), adj)

    weight_grad(t1, d2[1 : 1 + ROWS, 16 : 16 + COLS, :].reshape(ROWS * COLS, CH), 0, range(3))
    first = scatter_part(0, grads, line_in, sum_sems)

    @pl.loop(0, 4, unroll=4)
    def _(k):
        r = k * 4
        g = conv_rows(d2, w2f[...], r, 4, 1) * s1[pl.ds(r + 2, 4)].reshape(4 * WIDE, CH)
        d1[pl.ds(r, 4)] = g.reshape(4, WIDE, CH)[:, 16 : 16 + COLS].astype(BF)

    d1_all = d1[...].reshape(ROWS * COLS, CH)
    weight_grad(t0, d1_all, ONE, range(0, 2))
    first += scatter_part(1, grads, line_in, sum_sems)
    weight_grad(t0, d1_all, ONE, range(2, 3))
    first += scatter_part(2, grads, line_in, sum_sems)

    sum_all(first, grads, total, line_in, line_sum, plane_in, plane_sum, gathered, sum_sems)
    outs = []
    for i, (out, at, size) in enumerate(
        ((one_out, ONE, 9 * CH), (two_out, 0, 9 * CH), (rest_out, REST, 104))
    ):
        copy = pltpu.make_async_copy(total.at[at : at + size], out, out_sem.at[i])
        copy.start()
        outs.append(copy)
    for copy in outs:
        copy.wait()


def run_kernel(*args):
    vmem = pl.BlockSpec(memory_space=pltpu.VMEM)
    smem = pl.BlockSpec(memory_space=pltpu.SMEM)
    specs = [vmem] * 16
    specs[6] = smem
    specs[12] = smem
    dma = pltpu.SemaphoreType.DMA
    return pl.pallas_call(
        kernel,
        out_shape=(
            jax.ShapeDtypeStruct((9 * CH, CH), F32),
            jax.ShapeDtypeStruct((9 * CH, CH), F32),
            jax.ShapeDtypeStruct((104, CH), F32),
        ),
        in_specs=specs,
        out_specs=(pl.BlockSpec(memory_space=pl.ANY),) * 3,
        scratch_shapes=[
            pltpu.VMEM((ROWS + 6, WIDE, CH), BF),
            pltpu.VMEM((ROWS + 6, WIDE, CH), BF),
            pltpu.VMEM((ROWS + 4, WIDE, CH), BF),
            pltpu.VMEM((ROWS + 2, WIDE, CH), BF),
            pltpu.VMEM((ROWS + 4, WIDE, CH), F32),
            pltpu.VMEM((ROWS + 2, WIDE, CH), F32),
            pltpu.VMEM((3 * CH, 3 * CH), BF),
            pltpu.VMEM((3 * CH, 3 * CH), BF),
            pltpu.VMEM((3 * CH, 3 * CH), BF),
            pltpu.VMEM((3, ROWS, COLS), F32),
            pltpu.VMEM((2, 3, ROWS, COLS), F32),
            pltpu.VMEM((384, PIX), BF),
            pltpu.VMEM((8, PIX), F32),
            pltpu.VMEM((8, PIX), F32),
            pltpu.VMEM((96, VW), F32),
            pltpu.VMEM((VW, 9 * VW), BF),
            pltpu.VMEM((VW, 9 * VW), BF),
            pltpu.VMEM((32, PIX + 256), BF),
            pltpu.VMEM((3, VW, PIX + 256), BF),
            pltpu.VMEM((3, VW, PIX + 256), BF),
            pltpu.VMEM((VW, PIX), F32),
            pltpu.VMEM((72, PIX + 256), F32),
            pltpu.VMEM((3, 3, 8, 128), F32),
            pltpu.VMEM((3, 3, 24, 128), F32),
            pltpu.VMEM((3, ROWS, COLS), BF),
            pltpu.VMEM((8, 3, ROWS, COLS), BF),
            pltpu.VMEM((ROWS + 4, 32, 256), F32),
            pltpu.VMEM((ROWS + 4, 32, 256), F32),
            pltpu.VMEM((ROWS + 2, WIDE, CH), BF),
            pltpu.VMEM((ROWS, COLS, CH), BF),
            pltpu.VMEM((3, CH, (ROWS + 2) * COLS), BF),
            pltpu.VMEM((3, CH, (ROWS + 2) * COLS), BF),
            pltpu.VMEM((1, 512), F32),
            pltpu.VMEM((3, 32, CH), F32),
            pltpu.VMEM((2, ROWS * 8, CH), BF),
            pltpu.VMEM((2, ROWS * 8, CH), BF),
            pltpu.VMEM((GRAD_ROWS, CH), F32),
            pltpu.VMEM((GRAD_ROWS, CH), F32),
            pltpu.VMEM((3, 7, SHARE, CH), F32),
            pltpu.VMEM((3, 128, CH), F32),
            pltpu.VMEM((3, 15, 8, CH), F32),
            pltpu.VMEM((3, 8, CH), F32),
            pltpu.VMEM((3, 128, CH), F32),
            dma((8,)), dma((8,)), dma((2,)), dma((2,)), dma((2,)), dma((2,)), dma((8,)), dma((8,)), dma((3,)),
            dma((3,)), dma((3,)), dma((3,)), dma((3,)), dma((3,)), dma((3,)), dma((3,)), dma((3,)),
        ],
        compiler_params=pltpu.CompilerParams(
            collective_id=0, has_side_effects=True, vmem_limit_bytes=56 * 1024 * 1024
        ),
    )(*args)


def hand_over_kernel(one, two, rest, loss, one_out, two_out, grad_out, sems):
    copies = []
    for i, (src, dst) in enumerate(((one, one_out), (two, two_out))):
        copy = pltpu.make_async_copy(src, dst, sems.at[i])
        copy.start()
        copies.append(copy)
    for a in range(3):
        for b in range(3):
            grad_out[a, b] = rest[a * 32 + b * 8 : a * 32 + b * 8 + 3, :]
    loss[...] = rest[96:97, 0:1]
    for copy in copies:
        copy.wait()


def hand_over(one, two, rest):
    vmem, hbm = pl.BlockSpec(memory_space=pltpu.VMEM), pl.BlockSpec(memory_space=pl.ANY)
    block = jax.ShapeDtypeStruct((9 * CH, CH), F32)
    return pl.pallas_call(
        hand_over_kernel,
        out_shape=(
            jax.ShapeDtypeStruct((1, 1), F32),
            block,
            block,
            jax.ShapeDtypeStruct((3, 3, 3, CH), F32),
        ),
        in_specs=[vmem, vmem, vmem],
        out_specs=(vmem, hbm, hbm, vmem),
        scratch_shapes=[pltpu.SemaphoreType.DMA((2,))],
    )(one, two, rest)


def per_device(
    features,
    conv_one_w,
    conv_one_b,
    conv_two_w,
    conv_two_b,
    out_conv_w,
    out_conv_b,
    vgg_one_w,
    vgg_one_b,
    vgg_two_w,
    vgg_two_b,
    lin_weights,
    row_lists,
    tap_index,
    tap_weight,
    target_tiles,
):
    grad_one, grad_two, rest = run_kernel(
        features,
        conv_one_w,
        conv_one_b.reshape(1, CH),
        conv_two_w,
        conv_two_b.reshape(1, CH),
        jnp.transpose(out_conv_w, (0, 1, 3, 2)),
        out_conv_b,
        jnp.transpose(vgg_one_w, (1, 2, 3, 0)),
        vgg_one_b.reshape(1, VW),
        jnp.transpose(vgg_two_w, (2, 3, 0, 1)),
        vgg_two_b.reshape(1, VW),
        lin_weights.reshape(1, VW),
        jnp.transpose(row_lists, (1, 0, 2)),
        tap_index[0],
        tap_weight[0],
        target_tiles[0],
    )
    loss, grad_one, grad_two, grad_out = hand_over(grad_one, grad_two, rest)
    return (
        loss.reshape(()),
        grad_one.reshape(3, 3, CH, CH),
        grad_two.reshape(3, 3, CH, CH),
        jnp.transpose(grad_out, (0, 1, 3, 2)),
    )


def solution(mesh):
    in_specs = (
        P("grp", "lon", None),
        P(),
        P(),
        P(),
        P(),
        P(),
        P(),
        P(),
        P(),
        P(),
        P(),
        P(),
        P(("lon", "grp"), None, None),
        P(("lon", "grp"), None, None),
        P(("lon", "grp"), None, None),
        P(("lon", "grp"), None, None, None),
    )
    out_specs = (P(), P(), P(), P())
    return jax.shard_map(
        per_device, mesh=mesh, in_specs=in_specs, out_specs=out_specs, check_vma=False
    )
```
